256 devices in a mesh: ctx: 16 (over y, z_hi, core), ch: 16 (over z_lo, x).
Axes of the slice: x: 4, y: 4, z: 8 (z_hi: 2, z_lo: 4; z = z_hi * 4 + z_lo), core: 2. Of those that a mesh axis runs over, the one named last changes fastest.
Arguments:
- query: bfloat16 [16384, 2048], P('ctx', 'ch'), may hold values from -6 to 6
- key_in: bfloat16 [16384, 2048], P('ctx', 'ch'), may hold values from -6 to 6
- value: bfloat16 [16384, 2048], P('ctx', 'ch'), may hold values from -6 to 6
- short_taps: float32 [3, 3, 2048], P(None, None, 'ch'), may hold values from -3 to 3
- filt: float32 [16384, 2048], P('ctx', 'ch'), may hold values from -2 to 2
- skip_gain: float32 [2048], P('ch'), may hold values from -4 to 4
- out_weight: bfloat16 [2048, 2048], P('ch'), may hold values from -0.1875 to 0.1875
Outputs:
- mixed: bfloat16 [16384, 2048], P('ctx', 'ch')
The draws below stay inside these ranges and needn't reach their ends.
All inputs are finite; a program needn't handle non-finite values.
Results may differ from the reference program's by a relative error of at most 0.0049.
Values may be sent and summed in bfloat16 or wider, within the bound.
A program may use at most 64 MiB of HBM per device.

```python
import math
import jax
import jax.numpy as jnp
from jax import lax

CHANNELS = 2048
OUT_WIDTH = 2048
SEQ_LEN = 16384


def draw_filt(key, part):
    key = jax.random.fold_in(key, 7)
    keys = jax.random.split(key, 6)
    shape_full = (SEQ_LEN, CHANNELS)
    fast_share = 0.5
    stochastic_jitter = jax.random.truncated_normal(keys[0], -4.0, 4.0, shape_full, jnp.float32)
    is_fast = jax.random.uniform(keys[1], (CHANNELS,), jnp.float32) < fast_share
    fast_rate = 1.0 / jax.random.uniform(keys[2], (CHANNELS,), jnp.float32, 30.0, 50.0)
    low_log = math.log(0.1 / SEQ_LEN)
    high_log = math.log(1.5 / SEQ_LEN)
    slow_rate = jnp.exp(jax.random.uniform(keys[3], (CHANNELS,), jnp.float32, low_log, high_log))
    falloff_speed = jnp.where(is_fast, fast_rate, slow_rate)
    lag_offsets = jnp.arange(SEQ_LEN, dtype=jnp.float32)[:, None]
    flagged_indices = jax.random.randint(keys[4], (4,), 0, SEQ_LEN).astype(jnp.float32)
    removed_indices = jax.random.uniform(keys[5], (4,), jnp.float32, 0.5, 0.8)
    pulse_height = jnp.prod(jnp.where(lag_offsets[:, :, None] >= flagged_indices, removed_indices, 1.0), axis=2)
    multiplier_gain = jnp.sqrt(2.0 * falloff_speed / (1.0 - jnp.exp(-2.0 * falloff_speed * SEQ_LEN)))
    return (stochastic_jitter * jnp.exp(-falloff_speed * lag_offsets) * pulse_height * multiplier_gain).astype(jnp.float32)


def raised(values, key, source, target, parts, factor):
    owner, partner = [(jnp.arange(values.shape[position]) // (values.shape[position] // parts)).reshape([-1 if axis == position else 1 for axis in range(values.ndim)]) for position in (source, target)]
    chosen = jax.random.permutation(key, parts)[partner]
    strong = (owner == chosen) | (owner == (partner + parts // 2) % parts)
    return jnp.where(strong, factor * values, values)


def steps_of(own_key, shape, cuts, smallest, top_value):
    level = 1.0
    for axis_at, shards_of in cuts:
        draws = jax.random.uniform(jax.random.fold_in(jax.random.fold_in(own_key, 6), axis_at), (shards_of,), jnp.float32, smallest / len(cuts), top_value / len(cuts))
        level = level * jnp.repeat(jnp.exp(draws), shape[axis_at] // shards_of).reshape((-1,) + (1,) * (len(shape) - 1 - axis_at))
    return level


def centred(key, dims, spread, limit, cuts=(), held_as=jnp.bfloat16):
    gain = steps_of(key, dims, cuts, -0.22, 0.18) if cuts else 1.0
    entries = jax.random.normal(key, dims, jnp.float32) * spread * gain
    return jnp.minimum(jnp.maximum(entries, -limit), limit).astype(held_as)


def gaussian_with(stream_key, dims, width, bound, cuts, heavy, kind=jnp.bfloat16):
    result = width * jax.random.normal(stream_key, dims, jnp.float32)
    if cuts:
        result = result * steps_of(stream_key, dims, cuts, -0.22, 0.18)
    return jnp.clip(raised(result, jax.random.fold_in(stream_key, 3), *heavy), -bound, bound).astype(kind)


def setup_inputs(seed: int = 0) -> dict:
    streams_of = jax.random.split(jax.random.key(seed), 8)
    query = centred(streams_of[0], (SEQ_LEN, CHANNELS), 1.0, 6.0, ((0, 16), (1, 16)))
    key_in = centred(streams_of[1], (SEQ_LEN, CHANNELS), 1.0, 6.0, ((0, 16), (1, 16)))
    value = centred(streams_of[2], (SEQ_LEN, CHANNELS), 1.0, 6.0, ((0, 16), (1, 16)))
    short_taps = centred(streams_of[3], (3, 3, CHANNELS), 0.6, 3.0, ((2, 16),), jnp.float32)
    filt = draw_filt(jax.random.fold_in(streams_of[7], 71), 0)
    skip_gain = centred(streams_of[5], (CHANNELS,), 1.0, 4.0, ((0, 16),), jnp.float32)
    out_weight = gaussian_with(streams_of[6], (CHANNELS, OUT_WIDTH), CHANNELS ** -0.5, 0.1875, ((0, 16),), (0, 1, 16, 2.0))
    return dict(query=query, key_in=key_in, value=value, short_taps=short_taps, filt=filt, skip_gain=skip_gain, out_weight=out_weight)


def smooth(signal, filters):
    padded = jnp.pad(signal, ((2, 0), (0, 0)))
    return filters[0] * padded[2:] + filters[1] * padded[1:-1] + filters[2] * padded[:-2]


def reference(query, key_in, value, short_taps, filt, skip_gain, out_weight):
    gate_part = smooth(query.astype(jnp.float32), short_taps[:, 0, :])
    key_part = smooth(key_in.astype(jnp.float32), short_taps[:, 1, :])
    value_part = smooth(value.astype(jnp.float32), short_taps[:, 2, :])
    product = key_part * value_part
    width_block = math.gcd(CHANNELS, 256)
    groups = CHANNELS // width_block
    signal_blocks = product.reshape(SEQ_LEN, groups, width_block).transpose(1, 0, 2)
    filter_blocks = filt.reshape(SEQ_LEN, groups, width_block).transpose(1, 0, 2)

    def long_conv(paired):
        signal, response = paired
        spectrum = jnp.fft.rfft(signal, n=2 * SEQ_LEN, axis=0) * jnp.fft.rfft(response, n=2 * SEQ_LEN, axis=0)
        return jnp.fft.irfft(spectrum, n=2 * SEQ_LEN, axis=0)[:SEQ_LEN].astype(jnp.float32)

    conv = lax.map(long_conv, (signal_blocks, filter_blocks))
    conv = conv.transpose(1, 0, 2).reshape(SEQ_LEN, CHANNELS)
    hidden = (gate_part * (conv + skip_gain * product)).astype(jnp.bfloat16)
    return jnp.dot(hidden, out_weight, preferred_element_type=jnp.float32).astype(jnp.bfloat16)
```

```python
import functools

import jax
import jax.numpy as jnp
import ml_dtypes
import numpy as np
from jax import lax
from jax.experimental import pallas as pl
from jax.experimental.pallas import tpu as pltpu
from jax.sharding import PartitionSpec as P

CTX = 16
CH = 16
ROWS = 1024
LANES = 128
TILES = ROWS // 128
OWN = LANES // CTX
HALF = 1024
PIECE = TILES * OWN
F32 = jnp.float32
BF16 = jnp.bfloat16
MESH = pl.DeviceIdType.MESH


def hi_lo(matrix):
    high = matrix.astype(ml_dtypes.bfloat16)
    low = (matrix - high.astype(np.float64)).astype(ml_dtypes.bfloat16)
    return high, low


def transform_matrices():
    index = np.arange(128, dtype=np.float64)
    shifted = index + 0.25
    turn = 2.0 * np.pi
    first = turn * np.outer(shifted, index) / 128.0
    forward = np.concatenate([np.cos(first), -np.sin(first)], axis=0)
    first_hi, first_lo = hi_lo(forward)
    first_cat = np.concatenate([first_hi, first_lo], axis=1)
    twiddle = turn * np.outer(shifted, index) / 16384.0
    twiddles = np.stack([np.cos(twiddle), -np.sin(twiddle)]).astype(np.float32)
    second = turn * np.outer(index, index) / 128.0
    cos, sin = np.cos(second), np.sin(second)
    ahead = np.block([[cos, -sin], [sin, cos]])
    back = np.block([[cos, sin], [-sin, cos]])
    last = np.concatenate([np.cos(first).T, -np.sin(first).T], axis=1) / 16384.0
    squares = np.stack([first_cat, *hi_lo(ahead), *hi_lo(back)])
    finals = np.stack(hi_lo(last))
    return squares, finals, twiddles


def split(value):
    high = value.astype(BF16)
    return high, (value - high.astype(F32)).astype(BF16)


def mul(a, b):
    return jnp.dot(a, b, preferred_element_type=F32)


def spectrum_pair(load, squares, tw_re, tw_im):
    points = jnp.concatenate([load(0), load(1)], axis=1).astype(BF16)
    stage = mul(squares[0], jnp.concatenate([points, points], axis=0))
    parts = []
    for which in range(2):
        re = stage[:128, 128 * which : 128 * which + 128]
        im = stage[128:, 128 * which : 128 * which + 128]
        parts.append(jnp.concatenate([re * tw_re - im * tw_im, re * tw_im + im * tw_re], axis=1))
    high, low = split(jnp.concatenate(parts, axis=0))
    return mul(high, squares[1]) + mul(low, squares[1]) + mul(high, squares[2])


def inverse_pair(signal, response, squares, finals, tw_re, tw_im):
    s_re, s_im = signal[:, :128], signal[:, 128:]
    r_re, r_im = response[:, :128], response[:, 128:]
    high, low = split(
        jnp.concatenate([s_re * r_re - s_im * r_im, s_re * r_im + s_im * r_re], axis=1)
    )
    stage = mul(high, squares[3]) + mul(low, squares[3]) + mul(high, squares[4])
    turned = []
    for which in range(2):
        re = stage[128 * which : 128 * which + 128, :128]
        im = stage[128 * which : 128 * which + 128, 128:]
        turned.append(jnp.concatenate([re * tw_re + im * tw_im, im * tw_re - re * tw_im], axis=0))
    high, low = split(jnp.concatenate(turned, axis=1))
    both = mul(finals[0], high) + mul(finals[0], low) + mul(finals[1], high)
    return both[:, :128], both[:, 128:]


def kernel(
    q_hbm, k_hbm, v_hbm, taps_hbm, filt_hbm, skip_hbm, w_hbm, sq_hbm, fin_hbm, tw_hbm,
    out_hbm,
    q_in, k_in, v_in, taps, filt, skip, squares, finals, twiddle,
    ext, halo_out, halo_in, gate, product, stage, pieces, f_out, p_out, y_out, f_in, p_in, y_in,
    points, response, turned, hidden, hidden_in, weights, mixed,
    load_sem, halo_sem, send_sem, recv_sem, w_send, w_recv, core_send, core_recv,
    h_send, h_recv, o_send, o_recv,
):
    c, h = lax.axis_index("ctx"), lax.axis_index("ch")
    core = lax.rem(c, 2)
    sibling = c + 1 - 2 * core
    zb, at = h // 8, lax.rem(h, 8)
    za, x = at // 4, lax.rem(h, 4)
    across = (1 - zb) * 8 + at
    beside = zb * 8 + (1 - za) * 4 + x
    diagonal = (1 - zb) * 8 + (1 - za) * 4 + x

    loads = [
        pltpu.make_async_copy(src, dst, load_sem.at[i])
        for i, (src, dst) in enumerate(
            [
                (filt_hbm, filt), (k_hbm, k_in), (v_hbm, v_in), (q_hbm, q_in), (taps_hbm, taps),
                (skip_hbm, skip), (sq_hbm, squares), (fin_hbm, finals), (tw_hbm, twiddle),
                (w_hbm.at[pl.ds(0, 64), pl.ds(pl.multiple_of(zb * HALF, HALF), HALF)], weights.at[h, 0]),
                (w_hbm.at[pl.ds(64, 64), pl.ds(pl.multiple_of(zb * HALF, HALF), HALF)], weights.at[h, 1]),
            ]
        )
    ]
    for load in loads:
        load.start()

    barrier = pltpu.get_barrier_semaphore()

    @pl.loop(1, 16)
    def _(step):
        pl.semaphore_signal(
            barrier, inc=1, device_id={"ctx": lax.rem(c + step, CTX)}, device_id_type=MESH
        )
        pl.semaphore_signal(
            barrier, inc=1, device_id={"ch": lax.rem(h + step, CH)}, device_id_type=MESH
        )

    def to_pieces(tile, value):
        stage[:, OWN * tile : OWN * tile + OWN, :] = value.T.reshape(CTX, OWN, 128)

    def exchange(kind, source, target, step):
        peer = lax.rem(c + step, CTX)
        return pltpu.make_async_remote_copy(
            src_ref=source.at[peer], dst_ref=target.at[c], send_sem=send_sem.at[kind, peer],
            recv_sem=recv_sem.at[kind, c], device_id={"ctx": peer}, device_id_type=MESH,
        )

    def arrival(kind, source, target, step):
        peer = lax.rem(c + step, CTX)
        return pltpu.make_async_remote_copy(
            src_ref=source.at[peer], dst_ref=target.at[peer], send_sem=send_sem.at[kind, peer],
            recv_sem=recv_sem.at[kind, peer], device_id={"ctx": peer}, device_id_type=MESH,
        )

    def start_exchange(kind, source, target):
        @pl.loop(1, CTX)
        def _(step):
            exchange(kind, source, target, step).start()

        target[c] = source[c]

    def wait_exchange(kind, source, target):
        @pl.loop(1, CTX)
        def _(step):
            arrival(kind, source, target, step).wait_recv()

    def weight_copy(block, peer):
        return pltpu.make_async_remote_copy(
            src_ref=weights.at[block, core], dst_ref=weights.at[block, core],
            send_sem=w_send.at[block, peer], recv_sem=w_recv.at[block],
            device_id={"ch": peer}, device_id_type=MESH,
        )

    def weight_out():
        return pltpu.make_async_remote_copy(
            src_ref=w_hbm.at[
                pl.ds(pl.multiple_of(core * 64, 64), 64),
                pl.ds(pl.multiple_of((1 - zb) * HALF, HALF), HALF),
            ],
            dst_ref=weights.at[h, core],
            send_sem=w_send.at[h, across], recv_sem=w_recv.at[h],
            device_id={"ch": across}, device_id_type=MESH,
        )

    def along_x(block, step):
        return weight_copy(block, (h // 4) * 4 + lax.rem(x + step, 4))

    def send_along_x(block):
        @pl.loop(1, 4)
        def _(step):
            along_x(block, step).start()

    def core_copy(block):
        return pltpu.make_async_remote_copy(
            src_ref=weights.at[block, core], dst_ref=weights.at[block, core],
            send_sem=core_send.at[block], recv_sem=core_recv.at[block],
            device_id={"ctx": sibling}, device_id_type=MESH,
        )

    def core_arrival(block):
        return pltpu.make_async_remote_copy(
            src_ref=weights.at[block, 1 - core], dst_ref=weights.at[block, 1 - core],
            send_sem=core_send.at[block], recv_sem=core_recv.at[block],
            device_id={"ctx": sibling}, device_id_type=MESH,
        )

    loads[0].wait()
    for tile in range(TILES):
        to_pieces(tile, filt[128 * tile : 128 * tile + 128, :])
    f_out[...] = stage[...].astype(BF16)

    for load in loads[1:]:
        load.wait()
    for i, source in enumerate((k_in, v_in, q_in)):
        halo_out[16 * i : 16 * i + 16, :] = source[ROWS - 16 :, :]

    pl.semaphore_wait(barrier, 30)

    halo = pltpu.make_async_remote_copy(
        src_ref=halo_out, dst_ref=halo_in, send_sem=halo_sem.at[0], recv_sem=halo_sem.at[1],
        device_id={"ctx": lax.rem(c + 1, CTX)}, device_id_type=MESH,
    )
    halo.start()
    start_exchange(0, f_out, f_in)
    weight_out().start()
    weight_copy(h, beside).start()
    send_along_x(h)

    for i, source in enumerate((k_in, v_in, q_in)):
        ext[i, 8:, :] = source[...].astype(F32)

    def smooth(tile):
        first = 128 * tile + 8
        sums = []
        for i, which in enumerate((1, 2, 0)):
            total = taps[0, which : which + 1, :] * ext[i, first : first + 128, :]
            total += taps[1, which : which + 1, :] * ext[i, first - 1 : first + 127, :]
            total += taps[2, which : which + 1, :] * ext[i, first - 2 : first + 126, :]
            sums.append(total)
        both = sums[0] * sums[1]
        gate[tile] = sums[2]
        product[tile] = both
        to_pieces(tile, both)

    for tile in range(1, TILES):
        smooth(tile)
    halo.wait()
    for i in range(3):
        before = halo_in[16 * i : 16 * i + 16, :].astype(F32)[8:]
        ext[i, :8, :] = jnp.where(c == 0, jnp.zeros_like(before), before)
    smooth(0)
    p_out[...] = stage[...].astype(BF16)
    start_exchange(1, p_out, p_in)

    tw_re, tw_im = twiddle[0], twiddle[1]

    weight_copy(across, across).wait_recv()
    weight_copy(across, beside).start()
    send_along_x(across)
    weight_copy(beside, beside).wait_recv()
    send_along_x(beside)

    def gathered(source):
        points[...] = source[...].astype(F32).reshape(CTX * PIECE, 128)

    def loader(pair):
        return lambda which: points[pl.ds(2 * pair + which, 128, stride=OWN), :]

    wait_exchange(0, f_out, f_in)
    gathered(f_in)

    @pl.loop(0, OWN // 2)
    def _(pair):
        response[pair] = spectrum_pair(loader(pair), squares, tw_re, tw_im)

    weight_copy(diagonal, beside).wait_recv()
    send_along_x(diagonal)

    wait_exchange(1, p_out, p_in)
    gathered(p_in)

    @pl.loop(0, OWN // 2)
    def _(pair):
        signal = spectrum_pair(loader(pair), squares, tw_re, tw_im)
        low, high = inverse_pair(signal, response[pair], squares, finals, tw_re, tw_im)
        rows = pl.ds(pl.multiple_of(16 * pair, 16), 16)
        y_out[:, rows, :] = jnp.concatenate(
            [low.reshape(CTX, TILES, 128), high.reshape(CTX, TILES, 128)], axis=1
        ).astype(BF16)

    start_exchange(2, y_out, y_in)

    @pl.loop(1, 4)
    def _(step):
        peer_x = lax.rem(x + step, 4)

        @pl.loop(0, 4)
        def _(z):
            weight_copy(4 * z + peer_x, h).wait_recv()

    @pl.loop(1, CH)
    def _(step):
        core_copy(lax.rem(h + step, CH)).start()

    wait_exchange(2, y_out, y_in)
    turned[...] = y_in[...].astype(F32).reshape(CTX * PIECE, 128)

    def hidden_copy(half, tile):
        peer = 8 * half + tile
        return pltpu.make_async_remote_copy(
            src_ref=hidden.at[tile], dst_ref=hidden_in.at[h], send_sem=h_send.at[peer],
            recv_sem=h_recv.at[h], device_id={"ch": peer}, device_id_type=MESH,
        )

    @pl.loop(0, TILES)
    def _(step):
        tile = lax.rem(at + step, TILES)
        conv = turned[pl.ds(tile, 128, stride=TILES), :].T
        value = (gate[tile] * (conv + skip[...] * product[tile])).astype(BF16)
        hidden[tile] = value
        hidden_copy(1 - zb, tile).start()

        @pl.when(step == 0)
        def _():
            hidden_in[h] = value

        @pl.when(step > 0)
        def _():
            hidden_copy(zb, tile).start()

    @pl.loop(1, CH)
    def _(step):
        core_arrival(lax.rem(h + step, CH)).wait_recv()

    @pl.loop(1, CH)
    def _(step):
        peer = lax.rem(h + step, CH)
        pltpu.make_async_remote_copy(
            src_ref=hidden_in.at[peer], dst_ref=hidden_in.at[peer], send_sem=h_send.at[peer],
            recv_sem=h_recv.at[peer], device_id={"ch": peer}, device_id_type=MESH,
        ).wait_recv()

    lhs = jnp.concatenate([hidden_in[i] for i in range(CH)], axis=1)

    def mixed_copy(tile):
        return pltpu.make_async_remote_copy(
            src_ref=mixed.at[tile], dst_ref=out_hbm.at[pl.ds(pl.multiple_of(128 * at, 128), 128), :],
            send_sem=o_send.at[tile], recv_sem=o_recv.at[at],
            device_id={"ch": 8 * zb + tile}, device_id_type=MESH,
        )

    own_copy = pltpu.make_async_copy(
        mixed.at[at], out_hbm.at[pl.ds(pl.multiple_of(128 * at, 128), 128), :], load_sem.at[0]
    )

    for part in range(4):
        rhs = weights[:, :, :, 256 * part : 256 * part + 256].reshape(CH * LANES, 256)
        value = mul(lhs, rhs).astype(BF16)
        for i in range(2):
            tile = 2 * part + i
            mixed[tile] = value[:, 128 * i : 128 * i + 128]

            @pl.when(at != tile)
            def _():
                mixed_copy(tile).start()

            @pl.when(at == tile)
            def _():
                own_copy.start()

    @pl.loop(1, CTX)
    def _(step):
        arrival(0, f_out, f_in, step).wait_send()
        arrival(1, p_out, p_in, step).wait_send()
        arrival(2, y_out, y_in, step).wait_send()

    weight_out().wait_send()
    weight_copy(h, beside).wait_send()
    weight_copy(across, beside).wait_send()

    @pl.loop(1, 4)
    def _(step):
        along_x(h, step).wait_send()
        along_x(across, step).wait_send()
        along_x(beside, step).wait_send()
        along_x(diagonal, step).wait_send()

    @pl.loop(1, CH)
    def _(step):
        core_copy(lax.rem(h + step, CH)).wait_send()

    @pl.loop(0, TILES)
    def _(step):
        tile = lax.rem(at + step, TILES)
        hidden_copy(1 - zb, tile).wait_send()

        @pl.when(step > 0)
        def _():
            hidden_copy(zb, tile).wait_send()
            mixed_copy(tile).wait_send()
            pltpu.make_async_remote_copy(
                src_ref=mixed.at[tile],
                dst_ref=out_hbm.at[pl.ds(pl.multiple_of(128 * tile, 128), 128), :],
                send_sem=o_send.at[tile], recv_sem=o_recv.at[tile],
                device_id={"ch": 8 * zb + tile}, device_id_type=MESH,
            ).wait_recv()

    own_copy.wait()


def per_device(query, key_in, value, short_taps, filt, skip_gain, out_weight):
    squares, finals, twiddles = transform_matrices()
    any_space = pl.BlockSpec(memory_space=pl.ANY)
    dma = pltpu.SemaphoreType.DMA
    piece = (CTX, PIECE, 128)
    return pl.pallas_call(
        kernel,
        out_shape=jax.ShapeDtypeStruct((ROWS, LANES), BF16),
        in_specs=[any_space] * 10,
        out_specs=any_space,
        scratch_shapes=[
            pltpu.VMEM((ROWS, LANES), BF16),
            pltpu.VMEM((ROWS, LANES), BF16),
            pltpu.VMEM((ROWS, LANES), BF16),
            pltpu.VMEM((3, 3, LANES), F32),
            pltpu.VMEM((ROWS, LANES), F32),
            pltpu.VMEM((1, LANES), F32),
            pltpu.VMEM(squares.shape, BF16),
            pltpu.VMEM(finals.shape, BF16),
            pltpu.VMEM(twiddles.shape, F32),
            pltpu.VMEM((3, ROWS + 8, LANES), F32),
            pltpu.VMEM((48, LANES), BF16),
            pltpu.VMEM((48, LANES), BF16),
            pltpu.VMEM((TILES, 128, LANES), F32),
            pltpu.VMEM((TILES, 128, LANES), F32),
            pltpu.VMEM(piece, F32),
            pltpu.VMEM((8, 128), F32),
            pltpu.VMEM(piece, BF16),
            pltpu.VMEM(piece, BF16),
            pltpu.VMEM(piece, BF16),
            pltpu.VMEM(piece, BF16),
            pltpu.VMEM(piece, BF16),
            pltpu.VMEM(piece, BF16),
            pltpu.VMEM((CTX * PIECE, 128), F32),
            pltpu.VMEM((OWN // 2, 256, 256), F32),
            pltpu.VMEM((CTX * PIECE, 128), F32),
            pltpu.VMEM((TILES, 128, LANES), BF16),
            pltpu.VMEM((CH, 128, LANES), BF16),
            pltpu.VMEM((CH, 2, 64, HALF), BF16),
            pltpu.VMEM((TILES, 128, LANES), BF16),
            dma((11,)),
            dma((2,)),
            dma((3, CTX)),
            dma((3, CTX)),
            dma((CH, CH)),
            dma((CH,)),
            dma((CH,)),
            dma((CH,)),
            dma((CH,)),
            dma((CH,)),
            dma((TILES,)),
            dma((TILES,)),
        ],
        compiler_params=pltpu.CompilerParams(
            collective_id=0, has_side_effects=True, vmem_limit_bytes=40 * 1024 * 1024
        ),
        cost_estimate=pl.CostEstimate(flops=3_000_000_000, bytes_accessed=4_000_000, transcendentals=0),
    )(
        query, key_in, value, short_taps, filt, skip_gain.reshape(1, LANES), out_weight,
        jnp.asarray(squares), jnp.asarray(finals), jnp.asarray(twiddles),
    )


def solution(mesh):
    return jax.shard_map(
        per_device,
        mesh=mesh,
        in_specs=(
            P("ctx", "ch"),
            P("ctx", "ch"),
            P("ctx", "ch"),
            P(None, None, "ch"),
            P("ctx", "ch"),
            P("ch"),
            P("ch", None),
        ),
        out_specs=P("ctx", "ch"),
        check_vma=False,
    )
```

```python
import functools

import jax
import jax.numpy as jnp
import ml_dtypes
import numpy as np
from jax import lax
from jax.experimental import pallas as pl
from jax.experimental.pallas import tpu as pltpu
from jax.sharding import PartitionSpec as P

CTX = 16
CH = 16
ROWS = 1024
LANES = 128
TILES = ROWS // 128
OWN = LANES // CTX
HALF = 1024
GROUPS = 2
PART = LANES // GROUPS
MINE = OWN // GROUPS
PIECE = MINE * TILES
F32 = jnp.float32
BF16 = jnp.bfloat16
MESH = pl.DeviceIdType.MESH


def hi_lo(matrix):
    high = matrix.astype(ml_dtypes.bfloat16)
    low = (matrix - high.astype(np.float64)).astype(ml_dtypes.bfloat16)
    return high, low


def transform_matrices():
    index = np.arange(128, dtype=np.float64)
    shifted = index + 0.25
    turn = 2.0 * np.pi
    first = turn * np.outer(shifted, index) / 128.0
    forward = np.concatenate([np.cos(first), -np.sin(first)], axis=0)
    first_hi, first_lo = hi_lo(forward)
    first_cat = np.concatenate([first_hi, first_lo], axis=1)
    twiddle = turn * np.outer(shifted, index) / 16384.0
    twiddles = np.stack([np.cos(twiddle), -np.sin(twiddle)]).astype(np.float32)
    second = turn * np.outer(index, index) / 128.0
    cos, sin = np.cos(second), np.sin(second)
    ahead = np.block([[cos, -sin], [sin, cos]])
    back = np.block([[cos, sin], [-sin, cos]])
    last = np.concatenate([np.cos(first).T, -np.sin(first).T], axis=1) / 16384.0
    squares = np.stack([first_cat, *hi_lo(ahead), *hi_lo(back)])
    finals = np.stack(hi_lo(last))
    return squares, finals, twiddles


def split(value):
    high = value.astype(BF16)
    return high, (value - high.astype(F32)).astype(BF16)


def mul(a, b):
    return jnp.dot(a, b, preferred_element_type=F32)


def spectrum_pair(load, squares, tw_re, tw_im):
    points = jnp.concatenate([load(0), load(1)], axis=1).astype(BF16)
    stage = mul(squares[0], jnp.concatenate([points, points], axis=0))
    parts = []
    for which in range(2):
        re = stage[:128, 128 * which : 128 * which + 128]
        im = stage[128:, 128 * which : 128 * which + 128]
        parts.append(jnp.concatenate([re * tw_re - im * tw_im, re * tw_im + im * tw_re], axis=1))
    high, low = split(jnp.concatenate(parts, axis=0))
    return mul(high, squares[1]) + mul(low, squares[1]) + mul(high, squares[2])


def inverse_pair(signal, response, squares, finals, tw_re, tw_im):
    s_re, s_im = signal[:, :128], signal[:, 128:]
    r_re, r_im = response[:, :128], response[:, 128:]
    high, low = split(
        jnp.concatenate([s_re * r_re - s_im * r_im, s_re * r_im + s_im * r_re], axis=1)
    )
    stage = mul(high, squares[3]) + mul(low, squares[3]) + mul(high, squares[4])
    turned = []
    for which in range(2):
        re = stage[128 * which : 128 * which + 128, :128]
        im = stage[128 * which : 128 * which + 128, 128:]
        turned.append(jnp.concatenate([re * tw_re + im * tw_im, im * tw_re - re * tw_im], axis=0))
    high, low = split(jnp.concatenate(turned, axis=1))
    both = mul(finals[0], high) + mul(finals[0], low) + mul(finals[1], high)
    return both[:, :128], both[:, 128:]


def kernel(
    q_hbm, k_hbm, v_hbm, taps_hbm, filt_hbm, skip_hbm, w_hbm, sq_hbm, fin_hbm, tw_hbm,
    out_hbm,
    q_in, k_in, v_in, taps, filt, skip, squares, finals, twiddle,
    ext, halo_out, halo_in, filt_t, gate_t, product_t, skipped_t,
    f_out, p_out, y_out, f_in, p_in, y_in,
    response, rows_t, hidden, hidden_in, weights, lhs, total, mixed,
    load_sem, halo_sem, send_sem, recv_sem, w_send, w_recv, core_send, core_recv,
    h_send, h_recv, o_send, o_recv,
):
    c, h = lax.axis_index("ctx"), lax.axis_index("ch")
    core = lax.rem(c, 2)
    sibling = c + 1 - 2 * core
    zb, at = h // 8, lax.rem(h, 8)
    za, x = at // 4, lax.rem(h, 4)
    across = (1 - zb) * 8 + at
    beside = zb * 8 + (1 - za) * 4 + x
    diagonal = (1 - zb) * 8 + (1 - za) * 4 + x

    loads = [
        pltpu.make_async_copy(src, dst, load_sem.at[i])
        for i, (src, dst) in enumerate(
            [
                (filt_hbm, filt), (k_hbm, k_in), (v_hbm, v_in), (q_hbm, q_in), (taps_hbm, taps),
                (skip_hbm, skip), (sq_hbm, squares), (fin_hbm, finals), (tw_hbm, twiddle),
                (w_hbm.at[pl.ds(0, 64), pl.ds(pl.multiple_of(zb * HALF, HALF), HALF)], weights.at[h, 0]),
                (w_hbm.at[pl.ds(64, 64), pl.ds(pl.multiple_of(zb * HALF, HALF), HALF)], weights.at[h, 1]),
            ]
        )
    ]
    for load in loads:
        load.start()

    barrier = pltpu.get_barrier_semaphore()

    @pl.loop(1, 16)
    def _(step):
        pl.semaphore_signal(
            barrier, inc=1, device_id={"ctx": lax.rem(c + step, CTX)}, device_id_type=MESH
        )
        pl.semaphore_signal(
            barrier, inc=1, device_id={"ch": lax.rem(h + step, CH)}, device_id_type=MESH
        )

    def turn(target, tile, value):
        target[pl.ds(tile, LANES, stride=TILES), :] = value.T

    def pack(target, source):
        for g in range(GROUPS):
            rows = source[PART * TILES * g : PART * TILES * (g + 1), :]
            target[g] = rows.reshape(CTX, PIECE, 128).astype(BF16)

    def exchange(kind, g, source, target, step):
        peer = lax.rem(c + step, CTX)
        return pltpu.make_async_remote_copy(
            src_ref=source.at[g, peer], dst_ref=target.at[g, c],
            send_sem=send_sem.at[kind, g, peer], recv_sem=recv_sem.at[kind, g, c],
            device_id={"ctx": peer}, device_id_type=MESH,
        )

    def arrival(kind, g, source, target, step):
        peer = lax.rem(c + step, CTX)
        return pltpu.make_async_remote_copy(
            src_ref=source.at[g, peer], dst_ref=target.at[g, peer],
            send_sem=send_sem.at[kind, g, peer], recv_sem=recv_sem.at[kind, g, peer],
            device_id={"ctx": peer}, device_id_type=MESH,
        )

    def start_exchange(kind, g, source, target):
        @pl.loop(1, CTX)
        def _(step):
            exchange(kind, g, source, target, step).start()

        target[g, c] = source[g, c]

    def wait_exchange(kind, g, source, target):
        @pl.loop(1, CTX)
        def _(step):
            arrival(kind, g, source, target, step).wait_recv()

    def weight_copy(block, peer):
        return pltpu.make_async_remote_copy(
            src_ref=weights.at[block, core], dst_ref=weights.at[block, core],
            send_sem=w_send.at[block, peer], recv_sem=w_recv.at[block],
            device_id={"ch": peer}, device_id_type=MESH,
        )

    def weight_out():
        return pltpu.make_async_remote_copy(
            src_ref=w_hbm.at[
                pl.ds(pl.multiple_of(core * 64, 64), 64),
                pl.ds(pl.multiple_of((1 - zb) * HALF, HALF), HALF),
            ],
            dst_ref=weights.at[h, core],
            send_sem=w_send.at[h, across], recv_sem=w_recv.at[h],
            device_id={"ch": across}, device_id_type=MESH,
        )

    def along_x(block, step):
        return weight_copy(block, (h // 4) * 4 + lax.rem(x + step, 4))

    def send_along_x(block):
        @pl.loop(1, 4)
        def _(step):
            along_x(block, step).start()

    def core_copy(block):
        return pltpu.make_async_remote_copy(
            src_ref=weights.at[block, core], dst_ref=weights.at[block, core],
            send_sem=core_send.at[block], recv_sem=core_recv.at[block],
            device_id={"ctx": sibling}, device_id_type=MESH,
        )

    def core_arrival(block):
        return pltpu.make_async_remote_copy(
            src_ref=weights.at[block, 1 - core], dst_ref=weights.at[block, 1 - core],
            send_sem=core_send.at[block], recv_sem=core_recv.at[block],
            device_id={"ctx": sibling}, device_id_type=MESH,
        )

    loads[0].wait()
    for tile in range(TILES):
        turn(filt_t, tile, filt[128 * tile : 128 * tile + 128, :])
    pack(f_out, filt_t)

    for load in loads[1:]:
        load.wait()
    for i, source in enumerate((k_in, v_in, q_in)):
        halo_out[16 * i : 16 * i + 16, :] = source[ROWS - 16 :, :]
        ext[i, 8:, :] = source[...].astype(F32)

    def smooth(tile):
        first = 128 * tile + 8
        sums = []
        for i, which in enumerate((1, 2, 0)):
            part = taps[0, which : which + 1, :] * ext[i, first : first + 128, :]
            part += taps[1, which : which + 1, :] * ext[i, first - 1 : first + 127, :]
            part += taps[2, which : which + 1, :] * ext[i, first - 2 : first + 126, :]
            sums.append(part)
        both = sums[0] * sums[1]
        turn(product_t, tile, both)
        turn(skipped_t, tile, skip[...] * both)
        turn(gate_t, tile, sums[2])

    for tile in range(1, TILES):
        smooth(tile)

    pl.semaphore_wait(barrier, 30)

    halo = pltpu.make_async_remote_copy(
        src_ref=halo_out, dst_ref=halo_in, send_sem=halo_sem.at[0], recv_sem=halo_sem.at[1],
        device_id={"ctx": lax.rem(c + 1, CTX)}, device_id_type=MESH,
    )
    halo.start()
    for g in range(GROUPS):
        start_exchange(0, g, f_out, f_in)
    weight_out().start()
    weight_copy(h, beside).start()
    send_along_x(h)

    halo.wait()
    for i in range(3):
        before = halo_in[16 * i : 16 * i + 16, :].astype(F32)[8:]
        ext[i, :8, :] = jnp.where(c == 0, jnp.zeros_like(before), before)
    smooth(0)
    pack(p_out, product_t)
    for g in range(GROUPS):
        start_exchange(1, g, p_out, p_in)

    weight_copy(across, across).wait_recv()
    weight_copy(across, beside).start()
    send_along_x(across)
    weight_copy(beside, beside).wait_recv()
    send_along_x(beside)

    tw_re, tw_im = twiddle[0], twiddle[1]

    def loader(source, g, pair):
        both = source[g, :, 16 * pair : 16 * pair + 16, :].astype(F32)
        return lambda which: both[:, 8 * which : 8 * which + 8, :].reshape(128, 128)

    for g in range(GROUPS):
        wait_exchange(0, g, f_out, f_in)
        for pair in range(MINE // 2):
            response[g, pair] = spectrum_pair(loader(f_in, g, pair), squares, tw_re, tw_im)

    weight_copy(diagonal, beside).wait_recv()
    send_along_x(diagonal)

    for g in range(GROUPS):
        wait_exchange(1, g, p_out, p_in)
        for pair in range(MINE // 2):
            signal = spectrum_pair(loader(p_in, g, pair), squares, tw_re, tw_im)
            low, high = inverse_pair(signal, response[g, pair], squares, finals, tw_re, tw_im)
            y_out[g, :, 16 * pair : 16 * pair + 16, :] = jnp.concatenate(
                [low.reshape(CTX, TILES, 128), high.reshape(CTX, TILES, 128)], axis=1
            ).astype(BF16)
        start_exchange(2, g, y_out, y_in)

    def hidden_copy(g, half, tile):
        peer = 8 * half + tile
        return pltpu.make_async_remote_copy(
            src_ref=hidden.at[g, tile], dst_ref=hidden_in.at[g, h],
            send_sem=h_send.at[g, peer], recv_sem=h_recv.at[g, h],
            device_id={"ch": peer}, device_id_type=MESH,
        )

    for g in range(GROUPS):
        wait_exchange(2, g, y_out, y_in)
        for quarter in range(4):
            rows = slice(PART * TILES // 4 * quarter, PART * TILES // 4 * (quarter + 1))
            whole = slice(PART * TILES * g + rows.start, PART * TILES * g + rows.stop)
            conv = y_in[g, 4 * quarter : 4 * quarter + 4].astype(F32).reshape(4 * PIECE, 128)
            rows_t[rows, :] = gate_t[whole, :] * (conv + skipped_t[whole, :])

        @pl.loop(0, TILES)
        def _(step):
            tile = lax.rem(at + step, TILES)
            value = rows_t[pl.ds(tile, PART, stride=TILES), :].astype(BF16)
            hidden[g, tile] = value
            hidden_copy(g, 1 - zb, tile).start()

            @pl.when(step == 0)
            def _():
                hidden_in[g, h] = value

            @pl.when(step > 0)
            def _():
                hidden_copy(g, zb, tile).start()

    @pl.loop(1, 4)
    def _(step):
        peer_x = lax.rem(x + step, 4)

        @pl.loop(0, 4)
        def _(z):
            weight_copy(4 * z + peer_x, h).wait_recv()

    @pl.loop(1, CH)
    def _(step):
        core_copy(lax.rem(h + step, CH)).start()

    @pl.loop(1, CH)
    def _(step):
        core_arrival(lax.rem(h + step, CH)).wait_recv()

    def mixed_copy(tile):
        return pltpu.make_async_remote_copy(
            src_ref=mixed.at[tile], dst_ref=out_hbm.at[pl.ds(pl.multiple_of(128 * at, 128), 128), :],
            send_sem=o_send.at[tile], recv_sem=o_recv.at[at],
            device_id={"ch": 8 * zb + tile}, device_id_type=MESH,
        )

    own_copy = pltpu.make_async_copy(
        mixed.at[at], out_hbm.at[pl.ds(pl.multiple_of(128 * at, 128), 128), :], load_sem.at[0]
    )

    for g in range(GROUPS):

        @pl.loop(1, CH)
        def _(step):
            peer = lax.rem(h + step, CH)
            pltpu.make_async_remote_copy(
                src_ref=hidden_in.at[g, peer], dst_ref=hidden_in.at[g, peer],
                send_sem=h_send.at[g, peer], recv_sem=h_recv.at[g, peer],
                device_id={"ch": peer}, device_id_type=MESH,
            ).wait_recv()

        for i in range(CH // 2):
            two = hidden_in[g, 2 * i : 2 * i + 2].astype(F32).reshape(128, 128)
            lhs[:, 128 * i : 128 * i + 128] = two.T.astype(BF16)

        for part in range(4):
            cut = slice(256 * part, 256 * part + 256)
            value = mul(lhs[...], weights[:, g, :, cut].reshape(CH * PART, 256))
            if g < GROUPS - 1:
                total[:, cut] = value
                continue
            value = (total[:, cut] + value).astype(BF16)
            for i in range(2):
                tile = 2 * part + i
                mixed[tile] = value[:, 128 * i : 128 * i + 128]

                @pl.when(at != tile)
                def _():
                    mixed_copy(tile).start()

                @pl.when(at == tile)
                def _():
                    own_copy.start()

    for g in range(GROUPS):

        @pl.loop(1, CTX)
        def _(step):
            arrival(0, g, f_out, f_in, step).wait_send()
            arrival(1, g, p_out, p_in, step).wait_send()
            arrival(2, g, y_out, y_in, step).wait_send()

    weight_out().wait_send()
    weight_copy(h, beside).wait_send()
    weight_copy(across, beside).wait_send()

    @pl.loop(1, 4)
    def _(step):
        along_x(h, step).wait_send()
        along_x(across, step).wait_send()
        along_x(beside, step).wait_send()
        along_x(diagonal, step).wait_send()

    @pl.loop(1, CH)
    def _(step):
        core_copy(lax.rem(h + step, CH)).wait_send()

    @pl.loop(0, TILES)
    def _(step):
        tile = lax.rem(at + step, TILES)
        for g in range(GROUPS):
            hidden_copy(g, 1 - zb, tile).wait_send()

        @pl.when(step > 0)
        def _():
            for g in range(GROUPS):
                hidden_copy(g, zb, tile).wait_send()
            mixed_copy(tile).wait_send()
            pltpu.make_async_remote_copy(
                src_ref=mixed.at[tile],
                dst_ref=out_hbm.at[pl.ds(pl.multiple_of(128 * tile, 128), 128), :],
                send_sem=o_send.at[tile], recv_sem=o_recv.at[tile],
                device_id={"ch": 8 * zb + tile}, device_id_type=MESH,
            ).wait_recv()

    own_copy.wait()


def per_device(query, key_in, value, short_taps, filt, skip_gain, out_weight):
    squares, finals, twiddles = transform_matrices()
    in_hbm = pl.BlockSpec(memory_space=pltpu.HBM)
    dma = pltpu.SemaphoreType.DMA
    piece = (GROUPS, CTX, PIECE, 128)
    return pl.pallas_call(
        kernel,
        out_shape=jax.ShapeDtypeStruct((ROWS, LANES), BF16),
        in_specs=[in_hbm] * 10,
        out_specs=in_hbm,
        scratch_shapes=[
            pltpu.VMEM((ROWS, LANES), BF16),
            pltpu.VMEM((ROWS, LANES), BF16),
            pltpu.VMEM((ROWS, LANES), BF16),
            pltpu.VMEM((3, 3, LANES), F32),
            pltpu.VMEM((ROWS, LANES), F32),
            pltpu.VMEM((1, LANES), F32),
            pltpu.VMEM(squares.shape, BF16),
            pltpu.VMEM(finals.shape, BF16),
            pltpu.VMEM(twiddles.shape, F32),
            pltpu.VMEM((3, ROWS + 8, LANES), F32),
            pltpu.VMEM((48, LANES), BF16),
            pltpu.VMEM((48, LANES), BF16),
            pltpu.VMEM((ROWS, 128), F32),
            pltpu.VMEM((ROWS, 128), F32),
            pltpu.VMEM((ROWS, 128), F32),
            pltpu.VMEM((ROWS, 128), F32),
            pltpu.VMEM(piece, BF16),
            pltpu.VMEM(piece, BF16),
            pltpu.VMEM(piece, BF16),
            pltpu.VMEM(piece, BF16),
            pltpu.VMEM(piece, BF16),
            pltpu.VMEM(piece, BF16),
            pltpu.VMEM((GROUPS, MINE // 2, 256, 256), F32),
            pltpu.VMEM((PART * TILES, 128), F32),
            pltpu.VMEM((GROUPS, TILES, PART, 128), BF16),
            pltpu.VMEM((GROUPS, CH, PART, 128), BF16),
            pltpu.VMEM((CH, 2, 64, HALF), BF16),
            pltpu.VMEM((128, CH * PART), BF16),
            pltpu.VMEM((128, HALF), F32),
            pltpu.VMEM((TILES, 128, LANES), BF16),
            dma((11,)),
            dma((2,)),
            dma((3, GROUPS, CTX)),
            dma((3, GROUPS, CTX)),
            dma((CH, CH)),
            dma((CH,)),
            dma((CH,)),
            dma((CH,)),
            dma((GROUPS, CH)),
            dma((GROUPS, CH)),
            dma((TILES,)),
            dma((TILES,)),
        ],
        compiler_params=pltpu.CompilerParams(
            collective_id=0, has_side_effects=True, vmem_limit_bytes=60 * 1024 * 1024
        ),
        cost_estimate=pl.CostEstimate(flops=3_000_000_000, bytes_accessed=4_000_000, transcendentals=0),
    )(
        query, key_in, value, short_taps, filt, skip_gain.reshape(1, LANES), out_weight,
        jnp.asarray(squares), jnp.asarray(finals), jnp.asarray(twiddles),
    )


def solution(mesh):
    return jax.shard_map(
        per_device,
        mesh=mesh,
        in_specs=(
            P("ctx", "ch"),
            P("ctx", "ch"),
            P("ctx", "ch"),
            P(None, None, "ch"),
            P("ctx", "ch"),
            P("ch"),
            P("ch", None),
        ),
        out_specs=P("ctx", "ch"),
        check_vma=False,
    )
```

```python
import functools

import jax
import jax.numpy as jnp
import ml_dtypes
import numpy as np
from jax import lax
from jax.experimental import pallas as pl
from jax.experimental.pallas import tpu as pltpu
from jax.sharding import PartitionSpec as P

CTX = 16
CH = 16
ROWS = 1024
LANES = 128
TILES = ROWS // 128
OWN = LANES // CTX
HALF = 1024
GROUPS = 2
PART = LANES // GROUPS
MINE = OWN // GROUPS
PIECE = MINE * TILES
F32 = jnp.float32
BF16 = jnp.bfloat16
MESH = pl.DeviceIdType.MESH


def hi_lo(matrix):
    high = matrix.astype(ml_dtypes.bfloat16)
    low = (matrix - high.astype(np.float64)).astype(ml_dtypes.bfloat16)
    return high, low


def transform_matrices():
    index = np.arange(128, dtype=np.float64)
    shifted = index + 0.25
    turn = 2.0 * np.pi
    first = turn * np.outer(shifted, index) / 128.0
    forward = np.concatenate([np.cos(first), -np.sin(first)], axis=0)
    first_hi, first_lo = hi_lo(forward)
    first_cat = np.concatenate([first_hi, first_lo], axis=1)
    twiddle = turn * np.outer(shifted, index) / 16384.0
    twiddles = np.stack([np.cos(twiddle), -np.sin(twiddle)]).astype(np.float32)
    second = turn * np.outer(index, index) / 128.0
    cos, sin = np.cos(second), np.sin(second)
    ahead = np.block([[cos, -sin], [sin, cos]])
    back = np.block([[cos, sin], [-sin, cos]])
    last = np.concatenate([np.cos(first).T, -np.sin(first).T], axis=1) / 16384.0
    squares = np.stack([first_cat, *hi_lo(ahead), *hi_lo(back)])
    finals = np.stack(hi_lo(last))
    return squares, finals, twiddles


def split(value):
    high = value.astype(BF16)
    return high, (value - high.astype(F32)).astype(BF16)


def mul(a, b):
    return jnp.dot(a, b, preferred_element_type=F32)


def spectrum_pair(load, squares, tw_re, tw_im):
    points = jnp.concatenate([load(0), load(1)], axis=1).astype(BF16)
    stage = mul(squares[0], jnp.concatenate([points, points], axis=0))
    parts = []
    for which in range(2):
        re = stage[:128, 128 * which : 128 * which + 128]
        im = stage[128:, 128 * which : 128 * which + 128]
        parts.append(jnp.concatenate([re * tw_re - im * tw_im, re * tw_im + im * tw_re], axis=1))
    high, low = split(jnp.concatenate(parts, axis=0))
    return mul(high, squares[1]) + mul(low, squares[1]) + mul(high, squares[2])


def inverse_pair(signal, response, squares, finals, tw_re, tw_im):
    s_re, s_im = signal[:, :128], signal[:, 128:]
    r_re, r_im = response[:, :128], response[:, 128:]
    high, low = split(
        jnp.concatenate([s_re * r_re - s_im * r_im, s_re * r_im + s_im * r_re], axis=1)
    )
    stage = mul(high, squares[3]) + mul(low, squares[3]) + mul(high, squares[4])
    turned = []
    for which in range(2):
        re = stage[128 * which : 128 * which + 128, :128]
        im = stage[128 * which : 128 * which + 128, 128:]
        turned.append(jnp.concatenate([re * tw_re + im * tw_im, im * tw_re - re * tw_im], axis=0))
    high, low = split(jnp.concatenate(turned, axis=1))
    both = mul(finals[0], high) + mul(finals[0], low) + mul(finals[1], high)
    return both[:, :128], both[:, 128:]


def kernel(
    q_hbm, k_hbm, v_hbm, taps_hbm, filt_hbm, skip_hbm, w_hbm, sq_hbm, fin_hbm, tw_hbm,
    out_hbm,
    q_in, k_in, v_in, taps, filt, skip, squares, finals, twiddle,
    ext, halo_out, halo_in, filt_t, gate_t, product_t, skipped_t,
    f_out, p_out, y_out, f_in, p_in, y_in,
    response, rows_t, hidden, hidden_in, weights, lhs, total, mixed,
    load_sem, halo_sem, send_sem, recv_sem, z_send, w_send, w_recv, x_recv, core_send, core_recv,
    h_send, h_recv, o_send, o_recv,
):
    c, h = lax.axis_index("ctx"), lax.axis_index("ch")
    core = lax.rem(c, 2)
    sibling = c + 1 - 2 * core
    y = c // 4
    zb, at = h // 8, lax.rem(h, 8)
    za, x = at // 4, lax.rem(h, 4)
    across = (1 - zb) * 8 + at
    beside = zb * 8 + (1 - za) * 4 + x
    diagonal = (1 - zb) * 8 + (1 - za) * 4 + x

    loads = [
        pltpu.make_async_copy(src, dst, load_sem.at[i])
        for i, (src, dst) in enumerate(
            [
                (filt_hbm, filt), (k_hbm, k_in), (v_hbm, v_in), (q_hbm, q_in), (taps_hbm, taps),
                (skip_hbm, skip), (sq_hbm, squares), (fin_hbm, finals), (tw_hbm, twiddle),
                (w_hbm.at[pl.ds(0, 64), pl.ds(pl.multiple_of(zb * HALF, HALF), HALF)], weights.at[h, 0]),
                (w_hbm.at[pl.ds(64, 64), pl.ds(pl.multiple_of(zb * HALF, HALF), HALF)], weights.at[h, 1]),
            ]
        )
    ]
    for load in loads:
        load.start()

    barrier = pltpu.get_barrier_semaphore()

    @pl.loop(1, 16)
    def _(step):
        pl.semaphore_signal(
            barrier, inc=1, device_id={"ctx": lax.rem(c + step, CTX)}, device_id_type=MESH
        )
        pl.semaphore_signal(
            barrier, inc=1, device_id={"ch": lax.rem(h + step, CH)}, device_id_type=MESH
        )

    def turn(target, tile, value):
        target[pl.ds(tile, LANES, stride=TILES), :] = value.T

    def pack(target, source):
        for g in range(GROUPS):
            rows = source[PART * TILES * g : PART * TILES * (g + 1), :]
            target[g] = rows.reshape(CTX, PIECE, 128).astype(BF16)

    def exchange(kind, g, source, target, step):
        peer = lax.rem(c + step, CTX)
        return pltpu.make_async_remote_copy(
            src_ref=source.at[g, peer], dst_ref=target.at[g, c],
            send_sem=send_sem.at[kind, g, peer], recv_sem=recv_sem.at[kind, g, c],
            device_id={"ctx": peer}, device_id_type=MESH,
        )

    def arrival(kind, g, source, target, step):
        peer = lax.rem(c + step, CTX)
        return pltpu.make_async_remote_copy(
            src_ref=source.at[g, peer], dst_ref=target.at[g, peer],
            send_sem=send_sem.at[kind, g, peer], recv_sem=recv_sem.at[kind, g, peer],
            device_id={"ctx": peer}, device_id_type=MESH,
        )

    def start_exchange(kind, g, source, target):
        @pl.loop(1, CTX)
        def _(step):
            exchange(kind, g, source, target, step).start()

        target[g, c] = source[g, c]

    def wait_exchange(kind, g, source, target):
        @pl.loop(1, CTX)
        def _(step):
            arrival(kind, g, source, target, step).wait_recv()

    column = (h, across, beside, diagonal)

    def quarter(block, q):
        return weights.at[block, core, pl.ds(pl.multiple_of(16 * q, 16), 16)]

    def along_z(i):
        half = zb if i == 1 else 1 - zb
        return pltpu.make_async_remote_copy(
            src_ref=w_hbm.at[
                pl.ds(pl.multiple_of(core * 64 + y * 16, 16), 16),
                pl.ds(pl.multiple_of(half * HALF, HALF), HALF),
            ],
            dst_ref=quarter(h, y), send_sem=z_send.at[i], recv_sem=w_recv.at[h, y],
            device_id={"ch": column[i + 1]}, device_id_type=MESH,
        )

    def along_y(block, step):
        peer = lax.rem(y + step, 4)
        return pltpu.make_async_remote_copy(
            src_ref=quarter(block, y), dst_ref=quarter(block, y),
            send_sem=w_send.at[block, peer, 0], recv_sem=w_recv.at[block, y],
            device_id={"ctx": 4 * peer + lax.rem(c, 4)}, device_id_type=MESH,
        )

    def along_x(block, step, whole):
        peer = lax.rem(x + step, 4)
        part = weights.at[block, core] if whole else quarter(block, y)
        return pltpu.make_async_remote_copy(
            src_ref=part, dst_ref=part, send_sem=w_send.at[block, peer, 1],
            recv_sem=x_recv.at[block] if whole else w_recv.at[block, y],
            device_id={"ch": (h // 4) * 4 + peer}, device_id_type=MESH,
        )

    def wait_quarter(block, q):
        pltpu.make_async_remote_copy(
            src_ref=quarter(block, q), dst_ref=quarter(block, q),
            send_sem=w_send.at[block, 0, 0], recv_sem=w_recv.at[block, q],
            device_id={"ch": across}, device_id_type=MESH,
        ).wait_recv()

    def wait_whole(block):
        pltpu.make_async_remote_copy(
            src_ref=weights.at[block, core], dst_ref=weights.at[block, core],
            send_sem=w_send.at[block, 0, 0], recv_sem=x_recv.at[block],
            device_id={"ch": across}, device_id_type=MESH,
        ).wait_recv()

    def on_core(which):
        return pl.when(core == which)

    def steps_of_four(body):
        pl.loop(1, 4)(body)

    def other_columns(body):
        @pl.loop(1, 4)
        def _(step):
            peer = lax.rem(x + step, 4)

            @pl.loop(0, 4)
            def _(z):
                body(4 * z + peer)

    def weights_start():
        for i in range(3):
            along_z(i).start()

        @on_core(0)
        def _():
            steps_of_four(lambda step: along_x(h, step, True).start())

        @on_core(1)
        def _():
            steps_of_four(lambda step: along_x(h, step, False).start())

    def weights_second():
        for block in column[1:]:
            wait_quarter(block, y)

            @on_core(0)
            def _():
                steps_of_four(lambda step: along_y(block, step).start())

            @on_core(1)
            def _():
                steps_of_four(lambda step: along_x(block, step, False).start())

    def weights_third():
        @on_core(0)
        def _():
            for block in column[1:]:
                steps_of_four(lambda step: wait_quarter(block, lax.rem(y + step, 4)))
                steps_of_four(lambda step: along_x(block, step, True).start())

        @on_core(1)
        def _():
            for block in column[1:]:
                steps_of_four(lambda step: along_y(block, step).start())

            def onward(block):
                wait_quarter(block, y)
                steps_of_four(lambda step: along_y(block, step).start())

            other_columns(onward)

    def weights_gathered():
        @on_core(0)
        def _():
            other_columns(wait_whole)

        @on_core(1)
        def _():
            @pl.loop(1, CH)
            def _(step):
                block = lax.rem(h + step, CH)
                steps_of_four(lambda turn: wait_quarter(block, lax.rem(y + turn, 4)))

    def weights_drain():
        for i in range(3):
            along_z(i).wait_send()

        @on_core(0)
        def _():
            for block in column:
                steps_of_four(lambda step: along_x(block, step, True).wait_send())
            for block in column[1:]:
                steps_of_four(lambda step: along_y(block, step).wait_send())

        @on_core(1)
        def _():
            for block in column:
                steps_of_four(lambda step: along_x(block, step, False).wait_send())

            @pl.loop(1, CH)
            def _(step):
                block = lax.rem(h + step, CH)
                steps_of_four(lambda turn: along_y(block, turn).wait_send())

    def core_copy(block):
        return pltpu.make_async_remote_copy(
            src_ref=weights.at[block, core], dst_ref=weights.at[block, core],
            send_sem=core_send.at[block], recv_sem=core_recv.at[block],
            device_id={"ctx": sibling}, device_id_type=MESH,
        )

    def core_arrival(block):
        return pltpu.make_async_remote_copy(
            src_ref=weights.at[block, 1 - core], dst_ref=weights.at[block, 1 - core],
            send_sem=core_send.at[block], recv_sem=core_recv.at[block],
            device_id={"ctx": sibling}, device_id_type=MESH,
        )

    loads[0].wait()
    for tile in range(TILES):
        turn(filt_t, tile, filt[128 * tile : 128 * tile + 128, :])
    pack(f_out, filt_t)

    for load in loads[1:]:
        load.wait()
    for i, source in enumerate((k_in, v_in, q_in)):
        halo_out[16 * i : 16 * i + 16, :] = source[ROWS - 16 :, :]
        ext[i, 8:, :] = source[...].astype(F32)

    def smooth(tile):
        first = 128 * tile + 8
        sums = []
        for i, which in enumerate((1, 2, 0)):
            part = taps[0, which : which + 1, :] * ext[i, first : first + 128, :]
            part += taps[1, which : which + 1, :] * ext[i, first - 1 : first + 127, :]
            part += taps[2, which : which + 1, :] * ext[i, first - 2 : first + 126, :]
            sums.append(part)
        both = sums[0] * sums[1]
        turn(product_t, tile, both)
        turn(skipped_t, tile, skip[...] * both)
        turn(gate_t, tile, sums[2])

    for tile in range(1, TILES):
        smooth(tile)

    pl.semaphore_wait(barrier, 30)

    halo = pltpu.make_async_remote_copy(
        src_ref=halo_out, dst_ref=halo_in, send_sem=halo_sem.at[0], recv_sem=halo_sem.at[1],
        device_id={"ctx": lax.rem(c + 1, CTX)}, device_id_type=MESH,
    )
    halo.start()
    for g in range(GROUPS):
        start_exchange(0, g, f_out, f_in)
    weights_start()

    halo.wait()
    for i in range(3):
        before = halo_in[16 * i : 16 * i + 16, :].astype(F32)[8:]
        ext[i, :8, :] = jnp.where(c == 0, jnp.zeros_like(before), before)
    smooth(0)
    pack(p_out, product_t)
    for g in range(GROUPS):
        start_exchange(1, g, p_out, p_in)


    tw_re, tw_im = twiddle[0], twiddle[1]

    def loader(source, g, pair):
        both = source[g, :, 16 * pair : 16 * pair + 16, :].astype(F32)
        return lambda which: both[:, 8 * which : 8 * which + 8, :].reshape(128, 128)

    for g in range(GROUPS):
        wait_exchange(0, g, f_out, f_in)
        for pair in range(MINE // 2):
            response[g, pair] = spectrum_pair(loader(f_in, g, pair), squares, tw_re, tw_im)


    weights_second()
    for g in range(GROUPS):
        wait_exchange(1, g, p_out, p_in)
        for pair in range(MINE // 2):
            signal = spectrum_pair(loader(p_in, g, pair), squares, tw_re, tw_im)
            low, high = inverse_pair(signal, response[g, pair], squares, finals, tw_re, tw_im)
            y_out[g, :, 16 * pair : 16 * pair + 16, :] = jnp.concatenate(
                [low.reshape(CTX, TILES, 128), high.reshape(CTX, TILES, 128)], axis=1
            ).astype(BF16)
        start_exchange(2, g, y_out, y_in)

    weights_third()
    def hidden_copy(g, half, tile):
        peer = 8 * half + tile
        return pltpu.make_async_remote_copy(
            src_ref=hidden.at[g, tile], dst_ref=hidden_in.at[g, h],
            send_sem=h_send.at[g, peer], recv_sem=h_recv.at[g, h],
            device_id={"ch": peer}, device_id_type=MESH,
        )

    for g in range(GROUPS):
        wait_exchange(2, g, y_out, y_in)
        for fourth in range(4):
            rows = slice(PART * TILES // 4 * fourth, PART * TILES // 4 * (fourth + 1))
            whole = slice(PART * TILES * g + rows.start, PART * TILES * g + rows.stop)
            conv = y_in[g, 4 * fourth : 4 * fourth + 4].astype(F32).reshape(4 * PIECE, 128)
            rows_t[rows, :] = gate_t[whole, :] * (conv + skipped_t[whole, :])

        @pl.loop(0, TILES)
        def _(step):
            tile = lax.rem(at + step, TILES)
            value = rows_t[pl.ds(tile, PART, stride=TILES), :].astype(BF16)
            hidden[g, tile] = value
            hidden_copy(g, 1 - zb, tile).start()

            @pl.when(step == 0)
            def _():
                hidden_in[g, h] = value

            @pl.when(step > 0)
            def _():
                hidden_copy(g, zb, tile).start()

    weights_gathered()

    @pl.loop(1, CH)
    def _(step):
        core_copy(lax.rem(h + step, CH)).start()

    @pl.loop(1, CH)
    def _(step):
        core_arrival(lax.rem(h + step, CH)).wait_recv()

    def mixed_copy(tile):
        return pltpu.make_async_remote_copy(
            src_ref=mixed.at[tile], dst_ref=out_hbm.at[pl.ds(pl.multiple_of(128 * at, 128), 128), :],
            send_sem=o_send.at[tile], recv_sem=o_recv.at[at],
            device_id={"ch": 8 * zb + tile}, device_id_type=MESH,
        )

    own_copy = pltpu.make_async_copy(
        mixed.at[at], out_hbm.at[pl.ds(pl.multiple_of(128 * at, 128), 128), :], load_sem.at[0]
    )

    for g in range(GROUPS):

        @pl.loop(1, CH)
        def _(step):
            peer = lax.rem(h + step, CH)
            pltpu.make_async_remote_copy(
                src_ref=hidden_in.at[g, peer], dst_ref=hidden_in.at[g, peer],
                send_sem=h_send.at[g, peer], recv_sem=h_recv.at[g, peer],
                device_id={"ch": peer}, device_id_type=MESH,
            ).wait_recv()

        for i in range(CH // 2):
            two = hidden_in[g, 2 * i : 2 * i + 2].astype(F32).reshape(128, 128)
            lhs[:, 128 * i : 128 * i + 128] = two.T.astype(BF16)

        for part in range(4):
            cut = slice(256 * part, 256 * part + 256)
            value = mul(lhs[...], weights[:, g, :, cut].reshape(CH * PART, 256))
            if g < GROUPS - 1:
                total[:, cut] = value
                continue
            value = (total[:, cut] + value).astype(BF16)
            for i in range(2):
                tile = 2 * part + i
                mixed[tile] = value[:, 128 * i : 128 * i + 128]

                @pl.when(at != tile)
                def _():
                    mixed_copy(tile).start()

                @pl.when(at == tile)
                def _():
                    own_copy.start()

    for g in range(GROUPS):

        @pl.loop(1, CTX)
        def _(step):
            arrival(0, g, f_out, f_in, step).wait_send()
            arrival(1, g, p_out, p_in, step).wait_send()
            arrival(2, g, y_out, y_in, step).wait_send()

    weights_drain()

    @pl.loop(1, CH)
    def _(step):
        core_copy(lax.rem(h + step, CH)).wait_send()

    @pl.loop(0, TILES)
    def _(step):
        tile = lax.rem(at + step, TILES)
        for g in range(GROUPS):
            hidden_copy(g, 1 - zb, tile).wait_send()

        @pl.when(step > 0)
        def _():
            for g in range(GROUPS):
                hidden_copy(g, zb, tile).wait_send()
            mixed_copy(tile).wait_send()
            pltpu.make_async_remote_copy(
                src_ref=mixed.at[tile],
                dst_ref=out_hbm.at[pl.ds(pl.multiple_of(128 * tile, 128), 128), :],
                send_sem=o_send.at[tile], recv_sem=o_recv.at[tile],
                device_id={"ch": 8 * zb + tile}, device_id_type=MESH,
            ).wait_recv()

    own_copy.wait()


def per_device(query, key_in, value, short_taps, filt, skip_gain, out_weight):
    squares, finals, twiddles = transform_matrices()
    in_hbm = pl.BlockSpec(memory_space=pltpu.HBM)
    dma = pltpu.SemaphoreType.DMA
    piece = (GROUPS, CTX, PIECE, 128)
    return pl.pallas_call(
        kernel,
        out_shape=jax.ShapeDtypeStruct((ROWS, LANES), BF16),
        in_specs=[in_hbm] * 10,
        out_specs=in_hbm,
        scratch_shapes=[
            pltpu.VMEM((ROWS, LANES), BF16),
            pltpu.VMEM((ROWS, LANES), BF16),
            pltpu.VMEM((ROWS, LANES), BF16),
            pltpu.VMEM((3, 3, LANES), F32),
            pltpu.VMEM((ROWS, LANES), F32),
            pltpu.VMEM((1, LANES), F32),
            pltpu.VMEM(squares.shape, BF16),
            pltpu.VMEM(finals.shape, BF16),
            pltpu.VMEM(twiddles.shape, F32),
            pltpu.VMEM((3, ROWS + 8, LANES), F32),
            pltpu.VMEM((48, LANES), BF16),
            pltpu.VMEM((48, LANES), BF16),
            pltpu.VMEM((ROWS, 128), F32),
            pltpu.VMEM((ROWS, 128), F32),
            pltpu.VMEM((ROWS, 128), F32),
            pltpu.VMEM((ROWS, 128), F32),
            pltpu.VMEM(piece, BF16),
            pltpu.VMEM(piece, BF16),
            pltpu.VMEM(piece, BF16),
            pltpu.VMEM(piece, BF16),
            pltpu.VMEM(piece, BF16),
            pltpu.VMEM(piece, BF16),
            pltpu.VMEM((GROUPS, MINE // 2, 256, 256), F32),
            pltpu.VMEM((PART * TILES, 128), F32),
            pltpu.VMEM((GROUPS, TILES, PART, 128), BF16),
            pltpu.VMEM((GROUPS, CH, PART, 128), BF16),
            pltpu.VMEM((CH, 2, 64, HALF), BF16),
            pltpu.VMEM((128, CH * PART), BF16),
            pltpu.VMEM((128, HALF), F32),
            pltpu.VMEM((TILES, 128, LANES), BF16),
            dma((11,)),
            dma((2,)),
            dma((3, GROUPS, CTX)),
            dma((3, GROUPS, CTX)),
            dma((3,)),
            dma((CH, 4, 2)),
            dma((CH, 4)),
            dma((CH,)),
            dma((CH,)),
            dma((CH,)),
            dma((GROUPS, CH)),
            dma((GROUPS, CH)),
            dma((TILES,)),
            dma((TILES,)),
        ],
        compiler_params=pltpu.CompilerParams(
            collective_id=0, has_side_effects=True, vmem_limit_bytes=60 * 1024 * 1024
        ),
        cost_estimate=pl.CostEstimate(flops=3_000_000_000, bytes_accessed=4_000_000, transcendentals=0),
    )(
        query, key_in, value, short_taps, filt, skip_gain.reshape(1, LANES), out_weight,
        jnp.asarray(squares), jnp.asarray(finals), jnp.asarray(twiddles),
    )


def solution(mesh):
    return jax.shard_map(
        per_device,
        mesh=mesh,
        in_specs=(
            P("ctx", "ch"),
            P("ctx", "ch"),
            P("ctx", "ch"),
            P(None, None, "ch"),
            P("ctx", "ch"),
            P("ch"),
            P("ch", None),
        ),
        out_specs=P("ctx", "ch"),
        check_vma=False,
    )
```

```python
import functools

import jax
import jax.numpy as jnp
import ml_dtypes
import numpy as np
from jax import lax
from jax.experimental import pallas as pl
from jax.experimental.pallas import tpu as pltpu
from jax.sharding import PartitionSpec as P

CTX = 16
CH = 16
ROWS = 1024
LANES = 128
TILES = ROWS // 128
OWN = LANES // CTX
HALF = 1024
GROUPS = 2
PART = LANES // GROUPS
MINE = OWN // GROUPS
PIECE = MINE * TILES
F32 = jnp.float32
BF16 = jnp.bfloat16
MESH = pl.DeviceIdType.MESH


def hi_lo(matrix):
    high = matrix.astype(ml_dtypes.bfloat16)
    low = (matrix - high.astype(np.float64)).astype(ml_dtypes.bfloat16)
    return high, low


def transform_matrices():
    index = np.arange(128, dtype=np.float64)
    shifted = index + 0.25
    turn = 2.0 * np.pi
    first = turn * np.outer(shifted, index) / 128.0
    forward = np.concatenate([np.cos(first), -np.sin(first)], axis=0)
    first_hi, first_lo = hi_lo(forward)
    first_cat = np.concatenate([first_hi, first_lo], axis=1)
    twiddle = turn * np.outer(shifted, index) / 16384.0
    twiddles = np.stack([np.cos(twiddle), -np.sin(twiddle)]).astype(np.float32)
    second = turn * np.outer(index, index) / 128.0
    cos, sin = np.cos(second), np.sin(second)
    ahead = np.block([[cos, -sin], [sin, cos]])
    back = np.block([[cos, sin], [-sin, cos]])
    last = np.concatenate([np.cos(first).T, -np.sin(first).T], axis=1) / 16384.0
    squares = np.stack([first_cat, *hi_lo(ahead), *hi_lo(back)])
    finals = np.stack(hi_lo(last))
    return squares, finals, twiddles


def split(value):
    high = value.astype(BF16)
    return high, (value - high.astype(F32)).astype(BF16)


def mul(a, b):
    return jnp.dot(a, b, preferred_element_type=F32)


def spectrum_pair(load, squares, tw_re, tw_im):
    points = jnp.concatenate([load(0), load(1)], axis=1).astype(BF16)
    stage = mul(squares[0], jnp.concatenate([points, points], axis=0))
    parts = []
    for which in range(2):
        re = stage[:128, 128 * which : 128 * which + 128]
        im = stage[128:, 128 * which : 128 * which + 128]
        parts.append(jnp.concatenate([re * tw_re - im * tw_im, re * tw_im + im * tw_re], axis=1))
    high, low = split(jnp.concatenate(parts, axis=0))
    return mul(high, squares[1]) + mul(low, squares[1]) + mul(high, squares[2])


def inverse_pair(signal, response, squares, finals, tw_re, tw_im):
    s_re, s_im = signal[:, :128], signal[:, 128:]
    r_re, r_im = response[:, :128], response[:, 128:]
    high, low = split(
        jnp.concatenate([s_re * r_re - s_im * r_im, s_re * r_im + s_im * r_re], axis=1)
    )
    stage = mul(high, squares[3]) + mul(low, squares[3]) + mul(high, squares[4])
    turned = []
    for which in range(2):
        re = stage[128 * which : 128 * which + 128, :128]
        im = stage[128 * which : 128 * which + 128, 128:]
        turned.append(jnp.concatenate([re * tw_re + im * tw_im, im * tw_re - re * tw_im], axis=0))
    high, low = split(jnp.concatenate(turned, axis=1))
    both = mul(finals[0], high) + mul(finals[0], low) + mul(finals[1], high)
    return both[:, :128], both[:, 128:]


def kernel(
    q_hbm, k_hbm, v_hbm, taps_hbm, filt_hbm, skip_hbm, w_hbm, sq_hbm, fin_hbm, tw_hbm,
    out_hbm,
    q_in, k_in, v_in, taps, filt, skip, squares, finals, twiddle,
    ext, halo_out, halo_in, filt_t, gate_t, product_t, skipped_t,
    f_out, p_out, y_out, f_in, p_in, y_in,
    response, rows_t, hidden, hidden_in, weights, lhs, total, mixed,
    load_sem, halo_sem, send_sem, recv_sem, w_send, w_recv, y_recv, x_recv, core_send, core_recv,
    h_send, h_recv, o_send, o_recv,
):
    c, h = lax.axis_index("ctx"), lax.axis_index("ch")
    core = lax.rem(c, 2)
    sibling = c + 1 - 2 * core
    y = c // 4
    zb, at = h // 8, lax.rem(h, 8)
    za, x = at // 4, lax.rem(h, 4)
    across = (1 - zb) * 8 + at
    beside = zb * 8 + (1 - za) * 4 + x
    diagonal = (1 - zb) * 8 + (1 - za) * 4 + x

    loads = [
        pltpu.make_async_copy(src, dst, load_sem.at[i])
        for i, (src, dst) in enumerate(
            [
                (filt_hbm, filt), (k_hbm, k_in), (v_hbm, v_in), (q_hbm, q_in), (taps_hbm, taps),
                (skip_hbm, skip), (sq_hbm, squares), (fin_hbm, finals), (tw_hbm, twiddle),
                (w_hbm.at[pl.ds(0, 64), pl.ds(pl.multiple_of(zb * HALF, HALF), HALF)], weights.at[h, 0]),
                (w_hbm.at[pl.ds(64, 64), pl.ds(pl.multiple_of(zb * HALF, HALF), HALF)], weights.at[h, 1]),
            ]
        )
    ]
    for load in loads:
        load.start()

    barrier = pltpu.get_barrier_semaphore()

    @pl.loop(1, 16)
    def _(step):
        pl.semaphore_signal(
            barrier, inc=1, device_id={"ctx": lax.rem(c + step, CTX)}, device_id_type=MESH
        )
        pl.semaphore_signal(
            barrier, inc=1, device_id={"ch": lax.rem(h + step, CH)}, device_id_type=MESH
        )

    def turn(target, tile, value):
        target[pl.ds(tile, LANES, stride=TILES), :] = value.T

    def pack(target, source):
        for g in range(GROUPS):
            rows = source[PART * TILES * g : PART * TILES * (g + 1), :]
            target[g] = rows.reshape(CTX, PIECE, 128).astype(BF16)

    def exchange(kind, g, source, target, step):
        peer = lax.rem(c + step, CTX)
        return pltpu.make_async_remote_copy(
            src_ref=source.at[g, peer], dst_ref=target.at[g, c],
            send_sem=send_sem.at[kind, g], recv_sem=recv_sem.at[kind, g],
            device_id={"ctx": peer}, device_id_type=MESH,
        )

    def sum_of(part, send, recv):
        return pltpu.make_async_remote_copy(
            src_ref=part, dst_ref=part, send_sem=send, recv_sem=recv,
            device_id={"ctx": sibling}, device_id_type=MESH,
        )

    def pieces(kind, g, target):
        return sum_of(target.at[g, pl.ds(0, CTX - 1)], send_sem.at[kind, g], recv_sem.at[kind, g])

    def start_exchange(kind, g, source, target):
        @pl.loop(1, CTX)
        def _(step):
            exchange(kind, g, source, target, step).start()

        target[g, c] = source[g, c]

    def wait_exchange(kind, g, target):
        pieces(kind, g, target).wait_recv()

    column = (h, across, beside, diagonal)

    def quarter(block, q):
        return weights.at[block, core, pl.ds(pl.multiple_of(16 * q, 16), 16)]

    def along_z(i):
        half = zb if i == 1 else 1 - zb
        return pltpu.make_async_remote_copy(
            src_ref=w_hbm.at[
                pl.ds(pl.multiple_of(core * 64 + y * 16, 16), 16),
                pl.ds(pl.multiple_of(half * HALF, HALF), HALF),
            ],
            dst_ref=quarter(h, y), send_sem=w_send.at[0], recv_sem=w_recv.at[h],
            device_id={"ch": column[i + 1]}, device_id_type=MESH,
        )

    def along_y(block, step, low):
        peer = lax.rem(y + step, 4)
        return pltpu.make_async_remote_copy(
            src_ref=quarter(block, y), dst_ref=quarter(block, y),
            send_sem=w_send.at[0], recv_sem=y_recv.at[block] if low else y_recv.at[y],
            device_id={"ctx": 4 * peer + lax.rem(c, 4)}, device_id_type=MESH,
        )

    def along_x(block, step, whole):
        peer = lax.rem(x + step, 4)
        part = weights.at[block, core] if whole else quarter(block, y)
        return pltpu.make_async_remote_copy(
            src_ref=part, dst_ref=part, send_sem=w_send.at[0],
            recv_sem=x_recv.at[0] if whole else w_recv.at[block],
            device_id={"ch": (h // 4) * 4 + peer}, device_id_type=MESH,
        )

    def wait_quarter(block):
        sum_of(quarter(block, y), w_send.at[0], w_recv.at[block]).wait_recv()

    def on_core(which):
        return pl.when(core == which)

    def steps_of_four(body):
        pl.loop(1, 4)(body)

    def other_columns(body):
        @pl.loop(1, 4)
        def _(step):
            peer = lax.rem(x + step, 4)

            @pl.loop(0, 4)
            def _(z):
                body(4 * z + peer)

    def weights_start():
        for i in range(3):
            along_z(i).start()

        @on_core(0)
        def _():
            steps_of_four(lambda step: along_x(h, step, True).start())

        @on_core(1)
        def _():
            steps_of_four(lambda step: along_x(h, step, False).start())

    def weights_second():
        for block in column[1:]:
            wait_quarter(block)

            @on_core(0)
            def _():
                steps_of_four(lambda step: along_y(block, step, True).start())

            @on_core(1)
            def _():
                steps_of_four(lambda step: along_x(block, step, False).start())

    def weights_third():
        @on_core(0)
        def _():
            for block in column[1:]:
                three = weights.at[block, core, pl.ds(0, 48)]
                sum_of(three, w_send.at[0], y_recv.at[block]).wait_recv()
                steps_of_four(lambda step: along_x(block, step, True).start())

        @on_core(1)
        def _():
            for block in column[1:]:
                steps_of_four(lambda step: along_y(block, step, False).start())

            def onward(block):
                wait_quarter(block)
                steps_of_four(lambda step: along_y(block, step, False).start())

            other_columns(onward)

    def weights_gathered():
        @on_core(0)
        def _():
            sum_of(weights.at[pl.ds(0, 12), core], w_send.at[0], x_recv.at[0]).wait_recv()

        @on_core(1)
        def _():
            @pl.loop(1, 4)
            def _(step):
                part = weights.at[pl.ds(0, CH - 1), core, pl.ds(0, 16)]
                sum_of(part, w_send.at[0], y_recv.at[lax.rem(y + step, 4)]).wait_recv()

    def weights_drain():
        sum_of(weights.at[pl.ds(0, CH - 1), core], w_send.at[0], x_recv.at[0]).wait_send()

    def core_copy(block):
        return pltpu.make_async_remote_copy(
            src_ref=weights.at[block, core], dst_ref=weights.at[block, core],
            send_sem=core_send.at[0], recv_sem=core_recv.at[0],
            device_id={"ctx": sibling}, device_id_type=MESH,
        )

    def core_sum():
        return sum_of(weights.at[pl.ds(0, CH - 1), 1 - core], core_send.at[0], core_recv.at[0])

    loads[0].wait()
    for tile in range(TILES):
        turn(filt_t, tile, filt[128 * tile : 128 * tile + 128, :])
    pack(f_out, filt_t)

    for load in loads[1:]:
        load.wait()
    for i, source in enumerate((k_in, v_in, q_in)):
        halo_out[16 * i : 16 * i + 16, :] = source[ROWS - 16 :, :]
        ext[i, 8:, :] = source[...].astype(F32)

    def smooth(tile):
        first = 128 * tile + 8
        sums = []
        for i, which in enumerate((1, 2, 0)):
            part = taps[0, which : which + 1, :] * ext[i, first : first + 128, :]
            part += taps[1, which : which + 1, :] * ext[i, first - 1 : first + 127, :]
            part += taps[2, which : which + 1, :] * ext[i, first - 2 : first + 126, :]
            sums.append(part)
        both = sums[0] * sums[1]
        turn(product_t, tile, both)
        turn(skipped_t, tile, skip[...] * both)
        turn(gate_t, tile, sums[2])

    for tile in range(1, TILES):
        smooth(tile)

    pl.semaphore_wait(barrier, 30)

    halo = pltpu.make_async_remote_copy(
        src_ref=halo_out, dst_ref=halo_in, send_sem=halo_sem.at[0], recv_sem=halo_sem.at[1],
        device_id={"ctx": lax.rem(c + 1, CTX)}, device_id_type=MESH,
    )
    halo.start()
    for g in range(GROUPS):
        start_exchange(0, g, f_out, f_in)
    weights_start()

    halo.wait()
    for i in range(3):
        before = halo_in[16 * i : 16 * i + 16, :].astype(F32)[8:]
        ext[i, :8, :] = jnp.where(c == 0, jnp.zeros_like(before), before)
    smooth(0)
    pack(p_out, product_t)
    for g in range(GROUPS):
        start_exchange(1, g, p_out, p_in)


    tw_re, tw_im = twiddle[0], twiddle[1]

    def loader(source, g, pair):
        both = source[g, :, 16 * pair : 16 * pair + 16, :].astype(F32)
        return lambda which: both[:, 8 * which : 8 * which + 8, :].reshape(128, 128)

    for g in range(GROUPS):
        wait_exchange(0, g, f_in)
        for pair in range(MINE // 2):
            response[g, pair] = spectrum_pair(loader(f_in, g, pair), squares, tw_re, tw_im)


    weights_second()
    for g in range(GROUPS):
        wait_exchange(1, g, p_in)
        for pair in range(MINE // 2):
            signal = spectrum_pair(loader(p_in, g, pair), squares, tw_re, tw_im)
            low, high = inverse_pair(signal, response[g, pair], squares, finals, tw_re, tw_im)
            y_out[g, :, 16 * pair : 16 * pair + 16, :] = jnp.concatenate(
                [low.reshape(CTX, TILES, 128), high.reshape(CTX, TILES, 128)], axis=1
            ).astype(BF16)
        start_exchange(2, g, y_out, y_in)

    weights_third()
    def hidden_copy(g, half, tile):
        peer = 8 * half + tile
        return pltpu.make_async_remote_copy(
            src_ref=hidden.at[g, tile], dst_ref=hidden_in.at[g, h],
            send_sem=h_send.at[g], recv_sem=h_recv.at[g],
            device_id={"ch": peer}, device_id_type=MESH,
        )

    for g in range(GROUPS):
        wait_exchange(2, g, y_in)
        for fourth in range(4):
            rows = slice(PART * TILES // 4 * fourth, PART * TILES // 4 * (fourth + 1))
            whole = slice(PART * TILES * g + rows.start, PART * TILES * g + rows.stop)
            conv = y_in[g, 4 * fourth : 4 * fourth + 4].astype(F32).reshape(4 * PIECE, 128)
            rows_t[rows, :] = gate_t[whole, :] * (conv + skipped_t[whole, :])

        @pl.loop(0, TILES)
        def _(step):
            tile = lax.rem(at + step, TILES)
            value = rows_t[pl.ds(tile, PART, stride=TILES), :].astype(BF16)
            hidden[g, tile] = value
            hidden_copy(g, 1 - zb, tile).start()

            @pl.when(step == 0)
            def _():
                hidden_in[g, h] = value

            @pl.when(step > 0)
            def _():
                hidden_copy(g, zb, tile).start()

    weights_gathered()

    @pl.loop(1, CH)
    def _(step):
        core_copy(lax.rem(h + step, CH)).start()

    core_sum().wait_recv()

    def mixed_copy(tile):
        return pltpu.make_async_remote_copy(
            src_ref=mixed.at[tile], dst_ref=out_hbm.at[pl.ds(pl.multiple_of(128 * at, 128), 128), :],
            send_sem=o_send.at[0], recv_sem=o_recv.at[0],
            device_id={"ch": 8 * zb + tile}, device_id_type=MESH,
        )

    own_copy = pltpu.make_async_copy(
        mixed.at[at], out_hbm.at[pl.ds(pl.multiple_of(128 * at, 128), 128), :], load_sem.at[0]
    )

    def hidden_sum(g):
        return sum_of(hidden_in.at[g, pl.ds(0, CH - 1)], h_send.at[g], h_recv.at[g])

    for g in range(GROUPS):
        hidden_sum(g).wait_recv()
        many = 128 // PART
        for i in range(CH // many):
            block = hidden_in[g, many * i : many * i + many].astype(F32).reshape(128, 128)
            lhs[:, 128 * i : 128 * i + 128] = block.T.astype(BF16)

        for part in range(4):
            cut = slice(256 * part, 256 * part + 256)
            side, first = 2 * g // GROUPS, PART * g % 64
            rhs = weights[:, side, first : first + PART, cut].reshape(CH * PART, 256)
            value = mul(lhs[...], rhs)
            if g > 0:
                value += total[:, cut]
            if g < GROUPS - 1:
                total[:, cut] = value
                continue
            value = value.astype(BF16)
            for i in range(2):
                tile = 2 * part + i
                mixed[tile] = value[:, 128 * i : 128 * i + 128]

                @pl.when(at != tile)
                def _():
                    mixed_copy(tile).start()

                @pl.when(at == tile)
                def _():
                    own_copy.start()

    for g in range(GROUPS):
        for kind, target in enumerate((f_in, p_in, y_in)):
            pieces(kind, g, target).wait_send()
        hidden_sum(g).wait_send()
    weights_drain()
    core_sum().wait_send()
    seven = sum_of(mixed.at[pl.ds(0, TILES - 1)], o_send.at[0], o_recv.at[0])
    seven.wait_send()
    seven.wait_recv()
    own_copy.wait()


def per_device(query, key_in, value, short_taps, filt, skip_gain, out_weight):
    squares, finals, twiddles = transform_matrices()
    in_hbm = pl.BlockSpec(memory_space=pltpu.HBM)
    dma = pltpu.SemaphoreType.DMA
    piece = (GROUPS, CTX, PIECE, 128)
    return pl.pallas_call(
        kernel,
        out_shape=jax.ShapeDtypeStruct((ROWS, LANES), BF16),
        in_specs=[in_hbm] * 10,
        out_specs=in_hbm,
        scratch_shapes=[
            pltpu.VMEM((ROWS, LANES), BF16),
            pltpu.VMEM((ROWS, LANES), BF16),
            pltpu.VMEM((ROWS, LANES), BF16),
            pltpu.VMEM((3, 3, LANES), F32),
            pltpu.VMEM((ROWS, LANES), F32),
            pltpu.VMEM((1, LANES), F32),
            pltpu.VMEM(squares.shape, BF16),
            pltpu.VMEM(finals.shape, BF16),
            pltpu.VMEM(twiddles.shape, F32),
            pltpu.VMEM((3, ROWS + 8, LANES), F32),
            pltpu.VMEM((48, LANES), BF16),
            pltpu.VMEM((48, LANES), BF16),
            pltpu.VMEM((ROWS, 128), F32),
            pltpu.VMEM((ROWS, 128), F32),
            pltpu.VMEM((ROWS, 128), F32),
            pltpu.VMEM((ROWS, 128), F32),
            pltpu.VMEM(piece, BF16),
            pltpu.VMEM(piece, BF16),
            pltpu.VMEM(piece, BF16),
            pltpu.VMEM(piece, BF16),
            pltpu.VMEM(piece, BF16),
            pltpu.VMEM(piece, BF16),
            pltpu.VMEM((GROUPS, MINE // 2, 256, 256), F32),
            pltpu.VMEM((PART * TILES, 128), F32),
            pltpu.VMEM((GROUPS, TILES, PART, 128), BF16),
            pltpu.VMEM((GROUPS, CH, PART, 128), BF16),
            pltpu.VMEM((CH, 2, 64, HALF), BF16),
            pltpu.VMEM((128, CH * PART), BF16),
            pltpu.VMEM((128, HALF), F32),
            pltpu.VMEM((TILES, 128, LANES), BF16),
            dma((11,)),
            dma((2,)),
            dma((3, GROUPS)),
            dma((3, GROUPS)),
            dma((1,)),
            dma((CH,)),
            dma((CH,)),
            dma((1,)),
            dma((1,)),
            dma((1,)),
            dma((GROUPS,)),
            dma((GROUPS,)),
            dma((1,)),
            dma((1,)),
        ],
        compiler_params=pltpu.CompilerParams(
            collective_id=0, has_side_effects=True, vmem_limit_bytes=60 * 1024 * 1024
        ),
        cost_estimate=pl.CostEstimate(flops=3_000_000_000, bytes_accessed=4_000_000, transcendentals=0),
    )(
        query, key_in, value, short_taps, filt, skip_gain.reshape(1, LANES), out_weight,
        jnp.asarray(squares), jnp.asarray(finals), jnp.asarray(twiddles),
    )


def solution(mesh):
    return jax.shard_map(
        per_device,
        mesh=mesh,
        in_specs=(
            P("ctx", "ch"),
            P("ctx", "ch"),
            P("ctx", "ch"),
            P(None, None, "ch"),
            P("ctx", "ch"),
            P("ch"),
            P("ch", None),
        ),
        out_specs=P("ctx", "ch"),
        check_vma=False,
    )
```

```python
import functools

import jax
import jax.numpy as jnp
import ml_dtypes
import numpy as np
from jax import lax
from jax.experimental import pallas as pl
from jax.experimental.pallas import tpu as pltpu
from jax.sharding import PartitionSpec as P

CTX = 16
CH = 16
ROWS = 1024
LANES = 128
TILES = ROWS // 128
OWN = LANES // CTX
HALF = 1024
GROUPS = 2
PART = LANES // GROUPS
MINE = OWN // GROUPS
PIECE = MINE * TILES
F32 = jnp.float32
BF16 = jnp.bfloat16
MESH = pl.DeviceIdType.MESH


def hi_lo(matrix):
    high = matrix.astype(ml_dtypes.bfloat16)
    low = (matrix - high.astype(np.float64)).astype(ml_dtypes.bfloat16)
    return high, low


def transform_matrices():
    index = np.arange(128, dtype=np.float64)
    shifted = index + 0.25
    turn = 2.0 * np.pi
    first = turn * np.outer(shifted, index) / 128.0
    forward = np.concatenate([np.cos(first), -np.sin(first)], axis=0)
    first_hi, first_lo = hi_lo(forward)
    first_cat = np.concatenate([first_hi, first_lo], axis=1)
    twiddle = turn * np.outer(shifted, index) / 16384.0
    twiddles = np.stack([np.cos(twiddle), -np.sin(twiddle)]).astype(np.float32)
    second = turn * np.outer(index, index) / 128.0
    cos, sin = np.cos(second), np.sin(second)
    ahead = np.block([[cos, -sin], [sin, cos]])
    back = np.block([[cos, sin], [-sin, cos]])
    last = np.concatenate([np.cos(first).T, -np.sin(first).T], axis=1) / 16384.0
    squares = np.stack([first_cat, *hi_lo(ahead), *hi_lo(back)])
    finals = np.stack(hi_lo(last))
    return squares, finals, twiddles


def split(value):
    high = value.astype(BF16)
    return high, (value - high.astype(F32)).astype(BF16)


def mul(a, b):
    return jnp.dot(a, b, preferred_element_type=F32)


def spectrum(channels, squares, tw_re, tw_im):
    points = jnp.concatenate(channels, axis=1).astype(BF16)
    stage = mul(squares[0], jnp.concatenate([points, points], axis=0))
    parts = []
    for i in range(len(channels)):
        re, im = stage[:128, 128 * i : 128 * i + 128], stage[128:, 128 * i : 128 * i + 128]
        parts.append(jnp.concatenate([re * tw_re - im * tw_im, re * tw_im + im * tw_re], axis=1))
    high, low = split(jnp.concatenate(parts, axis=0))
    return mul(high, squares[1]) + mul(low, squares[1]) + mul(high, squares[2])


def causal(signal, response, squares, finals, tw_re, tw_im):
    s_re, s_im = signal[:, :128], signal[:, 128:]
    r_re, r_im = response[:, :128], response[:, 128:]
    high, low = split(
        jnp.concatenate([s_re * r_re - s_im * r_im, s_re * r_im + s_im * r_re], axis=1)
    )
    stage = mul(high, squares[3]) + mul(low, squares[3]) + mul(high, squares[4])
    turned = []
    for i in range(signal.shape[0] // 128):
        re, im = stage[128 * i : 128 * i + 128, :128], stage[128 * i : 128 * i + 128, 128:]
        turned.append(jnp.concatenate([re * tw_re + im * tw_im, im * tw_re - re * tw_im], axis=0))
    high, low = split(jnp.concatenate(turned, axis=1))
    return mul(finals[0], high) + mul(finals[0], low) + mul(finals[1], high)


def kernel(
    q_hbm, k_hbm, v_hbm, taps_hbm, filt_hbm, skip_hbm, w_hbm, sq_hbm, fin_hbm, tw_hbm,
    out_hbm,
    q_in, k_in, v_in, taps, filt, skip, squares, finals, twiddle,
    ext, halo_out, halo_in, filt_t, gate_t, product_t, skipped_t,
    f_out, p_out, y_out, f_in, p_in, y_in,
    response, rows_t, hidden, hidden_in, weights, lhs, total, mixed,
    load_sem, halo_sem, send_sem, recv_sem, w_send, w_recv, y_recv, x_recv, core_send, core_recv,
    h_send, h_recv, o_send, o_recv,
):
    c, h = lax.axis_index("ctx"), lax.axis_index("ch")
    core = lax.rem(c, 2)
    sibling = c + 1 - 2 * core
    y = c // 4
    zb, at = h // 8, lax.rem(h, 8)
    za, x = at // 4, lax.rem(h, 4)
    across = (1 - zb) * 8 + at
    beside = zb * 8 + (1 - za) * 4 + x
    diagonal = (1 - zb) * 8 + (1 - za) * 4 + x

    loads = [
        pltpu.make_async_copy(src, dst, load_sem.at[i])
        for i, (src, dst) in enumerate(
            [
                (filt_hbm, filt), (k_hbm, k_in), (v_hbm, v_in), (q_hbm, q_in), (taps_hbm, taps),
                (skip_hbm, skip), (sq_hbm, squares), (fin_hbm, finals), (tw_hbm, twiddle),
                (w_hbm.at[pl.ds(0, 64), pl.ds(pl.multiple_of(zb * HALF, HALF), HALF)], weights.at[h, 0]),
                (w_hbm.at[pl.ds(64, 64), pl.ds(pl.multiple_of(zb * HALF, HALF), HALF)], weights.at[h, 1]),
            ]
        )
    ]
    loads[0].start()

    barrier = pltpu.get_barrier_semaphore()

    @pl.loop(1, 16)
    def _(step):
        pl.semaphore_signal(
            barrier, inc=1, device_id={"ctx": lax.rem(c + step, CTX)}, device_id_type=MESH
        )

    @pl.loop(1, 16)
    def _(step):
        pl.semaphore_signal(
            barrier, inc=1, device_id={"ch": lax.rem(h + step, CH)}, device_id_type=MESH
        )

    for load in loads[1:]:
        load.start()

    def turn(target, tile, value):
        target[pl.ds(tile, LANES, stride=TILES), :] = value.T

    def pack(target, source):
        for g in range(GROUPS):
            rows = source[PART * TILES * g : PART * TILES * (g + 1), :]
            target[g] = rows.reshape(CTX, PIECE, 128).astype(BF16)

    def exchange(kind, g, source, target, step):
        peer = lax.rem(c + step, CTX)
        return pltpu.make_async_remote_copy(
            src_ref=source.at[g, peer], dst_ref=target.at[g, c],
            send_sem=send_sem.at[kind, g], recv_sem=recv_sem.at[kind, g],
            device_id={"ctx": peer}, device_id_type=MESH,
        )

    def sum_of(part, send, recv):
        return pltpu.make_async_remote_copy(
            src_ref=part, dst_ref=part, send_sem=send, recv_sem=recv,
            device_id={"ctx": sibling}, device_id_type=MESH,
        )

    def pieces(kind, g, target):
        return sum_of(target.at[g, pl.ds(0, CTX - 1)], send_sem.at[kind, g], recv_sem.at[kind, g])

    def start_exchange(kind, g, source, target):
        @pl.loop(1, CTX)
        def _(step):
            exchange(kind, g, source, target, step).start()

        target[g, c] = source[g, c]

    def wait_exchange(kind, g, target):
        pieces(kind, g, target).wait_recv()

    column = (h, across, beside, diagonal)

    def quarter(block, q):
        return weights.at[block, core, pl.ds(pl.multiple_of(16 * q, 16), 16)]

    def along_z(i):
        half = zb if i == 1 else 1 - zb
        return pltpu.make_async_remote_copy(
            src_ref=w_hbm.at[
                pl.ds(pl.multiple_of(core * 64 + y * 16, 16), 16),
                pl.ds(pl.multiple_of(half * HALF, HALF), HALF),
            ],
            dst_ref=quarter(h, y), send_sem=w_send.at[0], recv_sem=w_recv.at[h],
            device_id={"ch": column[i + 1]}, device_id_type=MESH,
        )

    def along_y(block, step, low):
        peer = lax.rem(y + step, 4)
        return pltpu.make_async_remote_copy(
            src_ref=quarter(block, y), dst_ref=quarter(block, y),
            send_sem=w_send.at[0], recv_sem=y_recv.at[block] if low else y_recv.at[y],
            device_id={"ctx": 4 * peer + lax.rem(c, 4)}, device_id_type=MESH,
        )

    def along_x(block, step, whole):
        peer = lax.rem(x + step, 4)
        part = weights.at[block, core] if whole else quarter(block, y)
        return pltpu.make_async_remote_copy(
            src_ref=part, dst_ref=part, send_sem=w_send.at[0],
            recv_sem=x_recv.at[0] if whole else w_recv.at[block],
            device_id={"ch": (h // 4) * 4 + peer}, device_id_type=MESH,
        )

    def wait_quarter(block):
        sum_of(quarter(block, y), w_send.at[0], w_recv.at[block]).wait_recv()

    def on_core(which):
        return pl.when(core == which)

    def steps_of_four(body):
        pl.loop(1, 4)(body)

    def other_columns(body):
        @pl.loop(1, 4)
        def _(step):
            peer = lax.rem(x + step, 4)

            @pl.loop(0, 4)
            def _(z):
                body(4 * z + peer)

    def weights_start():
        for i in range(3):
            along_z(i).start()

        @on_core(0)
        def _():
            steps_of_four(lambda step: along_x(h, step, True).start())

        @on_core(1)
        def _():
            steps_of_four(lambda step: along_x(h, step, False).start())

    def weights_second():
        for block in column[1:]:
            wait_quarter(block)

            @on_core(0)
            def _():
                steps_of_four(lambda step: along_y(block, step, True).start())

            @on_core(1)
            def _():
                steps_of_four(lambda step: along_x(block, step, False).start())

    def weights_third():
        @on_core(0)
        def _():
            for block in column[1:]:
                three = weights.at[block, core, pl.ds(0, 48)]
                sum_of(three, w_send.at[0], y_recv.at[block]).wait_recv()
                steps_of_four(lambda step: along_x(block, step, True).start())

        @on_core(1)
        def _():
            for block in column[1:]:
                steps_of_four(lambda step: along_y(block, step, False).start())

            def onward(block):
                wait_quarter(block)
                steps_of_four(lambda step: along_y(block, step, False).start())

            other_columns(onward)

    def weights_gathered():
        @on_core(0)
        def _():
            sum_of(weights.at[pl.ds(0, 12), core], w_send.at[0], x_recv.at[0]).wait_recv()

        @on_core(1)
        def _():
            @pl.loop(1, 4)
            def _(step):
                part = weights.at[pl.ds(0, CH - 1), core, pl.ds(0, 16)]
                sum_of(part, w_send.at[0], y_recv.at[lax.rem(y + step, 4)]).wait_recv()

    def weights_drain():
        sum_of(weights.at[pl.ds(0, CH - 1), core], w_send.at[0], x_recv.at[0]).wait_send()

    def core_copy(block):
        return pltpu.make_async_remote_copy(
            src_ref=weights.at[block, core], dst_ref=weights.at[block, core],
            send_sem=core_send.at[0], recv_sem=core_recv.at[0],
            device_id={"ctx": sibling}, device_id_type=MESH,
        )

    def core_sum():
        return sum_of(weights.at[pl.ds(0, CH - 1), 1 - core], core_send.at[0], core_recv.at[0])

    loads[0].wait()
    for tile in range(TILES):
        turn(filt_t, tile, filt[128 * tile : 128 * tile + 128, :])
    pack(f_out, filt_t)

    for load in loads[1:]:
        load.wait()
    for i, source in enumerate((k_in, v_in, q_in)):
        halo_out[16 * i : 16 * i + 16, :] = source[ROWS - 16 :, :]
        ext[i, 8:, :] = source[...].astype(F32)

    def smooth(tile):
        first = 128 * tile + 8
        sums = []
        for i, which in enumerate((1, 2, 0)):
            part = taps[0, which : which + 1, :] * ext[i, first : first + 128, :]
            part += taps[1, which : which + 1, :] * ext[i, first - 1 : first + 127, :]
            part += taps[2, which : which + 1, :] * ext[i, first - 2 : first + 126, :]
            sums.append(part)
        both = sums[0] * sums[1]
        turn(product_t, tile, both)
        turn(skipped_t, tile, skip[...] * both)
        turn(gate_t, tile, sums[2])

    for tile in range(1, TILES):
        smooth(tile)

    pl.semaphore_wait(barrier, 30)

    halo = pltpu.make_async_remote_copy(
        src_ref=halo_out, dst_ref=halo_in, send_sem=halo_sem.at[0], recv_sem=halo_sem.at[1],
        device_id={"ctx": lax.rem(c + 1, CTX)}, device_id_type=MESH,
    )
    halo.start()
    for g in range(GROUPS):
        start_exchange(0, g, f_out, f_in)
    weights_start()

    halo.wait()
    for i in range(3):
        before = halo_in[16 * i : 16 * i + 16, :].astype(F32)[8:]
        ext[i, :8, :] = jnp.where(c == 0, jnp.zeros_like(before), before)
    smooth(0)
    pack(p_out, product_t)
    for g in range(GROUPS):
        start_exchange(1, g, p_out, p_in)


    tw_re, tw_im = twiddle[0], twiddle[1]

    def channels(source, g):
        parts = source[g].astype(F32)
        return [parts[:, 8 * i : 8 * i + 8, :].reshape(128, 128) for i in range(MINE)]

    for g in range(GROUPS):
        wait_exchange(0, g, f_in)
        response[g] = spectrum(channels(f_in, g), squares, tw_re, tw_im)

    weights_second()
    for g in range(GROUPS):
        wait_exchange(1, g, p_in)
        signal = spectrum(channels(p_in, g), squares, tw_re, tw_im)
        conv = causal(signal, response[g], squares, finals, tw_re, tw_im)
        rows = [conv[:, 128 * i : 128 * i + 128].reshape(CTX, TILES, 128) for i in range(MINE)]
        y_out[g] = jnp.concatenate(rows, axis=1).astype(BF16)
        start_exchange(2, g, y_out, y_in)

    weights_third()
    def hidden_copy(g, half, tile):
        peer = 8 * half + tile
        return pltpu.make_async_remote_copy(
            src_ref=hidden.at[g, tile], dst_ref=hidden_in.at[g, h],
            send_sem=h_send.at[g], recv_sem=h_recv.at[g],
            device_id={"ch": peer}, device_id_type=MESH,
        )

    for g in range(GROUPS):
        wait_exchange(2, g, y_in)
        for fourth in range(4):
            rows = slice(PART * TILES // 4 * fourth, PART * TILES // 4 * (fourth + 1))
            whole = slice(PART * TILES * g + rows.start, PART * TILES * g + rows.stop)
            conv = y_in[g, 4 * fourth : 4 * fourth + 4].astype(F32).reshape(4 * PIECE, 128)
            rows_t[rows, :] = gate_t[whole, :] * (conv + skipped_t[whole, :])

        @pl.loop(0, TILES)
        def _(step):
            tile = lax.rem(at + step, TILES)
            value = rows_t[pl.ds(tile, PART, stride=TILES), :].astype(BF16)
            hidden[g, tile] = value
            hidden_copy(g, 1 - zb, tile).start()

            @pl.when(step == 0)
            def _():
                hidden_in[g, h] = value

            @pl.when(step > 0)
            def _():
                hidden_copy(g, zb, tile).start()

    weights_gathered()

    @pl.loop(1, CH)
    def _(step):
        core_copy(lax.rem(h + step, CH)).start()

    core_sum().wait_recv()

    def mixed_copy(tile):
        return pltpu.make_async_remote_copy(
            src_ref=mixed.at[tile], dst_ref=out_hbm.at[pl.ds(pl.multiple_of(128 * at, 128), 128), :],
            send_sem=o_send.at[0], recv_sem=o_recv.at[0],
            device_id={"ch": 8 * zb + tile}, device_id_type=MESH,
        )

    own_copy = pltpu.make_async_copy(
        mixed.at[at], out_hbm.at[pl.ds(pl.multiple_of(128 * at, 128), 128), :], load_sem.at[0]
    )

    def hidden_sum(g):
        return sum_of(hidden_in.at[g, pl.ds(0, CH - 1)], h_send.at[g], h_recv.at[g])

    for g in range(GROUPS):
        hidden_sum(g).wait_recv()
        many = 128 // PART
        for i in range(CH // many):
            block = hidden_in[g, many * i : many * i + many].astype(F32).reshape(128, 128)
            lhs[:, 128 * i : 128 * i + 128] = block.T.astype(BF16)

        for part in range(4):
            cut = slice(256 * part, 256 * part + 256)
            side, first = 2 * g // GROUPS, PART * g % 64
            rhs = weights[:, side, first : first + PART, cut].reshape(CH * PART, 256)
            value = mul(lhs[...], rhs)
            if g > 0:
                value += total[:, cut]
            if g < GROUPS - 1:
                total[:, cut] = value
                continue
            value = value.astype(BF16)
            for i in range(2):
                tile = 2 * part + i
                mixed[tile] = value[:, 128 * i : 128 * i + 128]

                @pl.when(at != tile)
                def _():
                    mixed_copy(tile).start()

                @pl.when(at == tile)
                def _():
                    own_copy.start()

    for g in range(GROUPS):
        for kind, target in enumerate((f_in, p_in, y_in)):
            pieces(kind, g, target).wait_send()
        hidden_sum(g).wait_send()
    weights_drain()
    core_sum().wait_send()
    seven = sum_of(mixed.at[pl.ds(0, TILES - 1)], o_send.at[0], o_recv.at[0])
    seven.wait_send()
    seven.wait_recv()
    own_copy.wait()


def per_device(query, key_in, value, short_taps, filt, skip_gain, out_weight):
    squares, finals, twiddles = transform_matrices()
    in_hbm = pl.BlockSpec(memory_space=pltpu.HBM)
    dma = pltpu.SemaphoreType.DMA
    piece = (GROUPS, CTX, PIECE, 128)
    return pl.pallas_call(
        kernel,
        out_shape=jax.ShapeDtypeStruct((ROWS, LANES), BF16),
        in_specs=[in_hbm] * 10,
        out_specs=in_hbm,
        scratch_shapes=[
            pltpu.VMEM((ROWS, LANES), BF16),
            pltpu.VMEM((ROWS, LANES), BF16),
            pltpu.VMEM((ROWS, LANES), BF16),
            pltpu.VMEM((3, 3, LANES), F32),
            pltpu.VMEM((ROWS, LANES), F32),
            pltpu.VMEM((1, LANES), F32),
            pltpu.VMEM(squares.shape, BF16),
            pltpu.VMEM(finals.shape, BF16),
            pltpu.VMEM(twiddles.shape, F32),
            pltpu.VMEM((3, ROWS + 8, LANES), F32),
            pltpu.VMEM((48, LANES), BF16),
            pltpu.VMEM((48, LANES), BF16),
            pltpu.VMEM((ROWS, 128), F32),
            pltpu.VMEM((ROWS, 128), F32),
            pltpu.VMEM((ROWS, 128), F32),
            pltpu.VMEM((ROWS, 128), F32),
            pltpu.VMEM(piece, BF16),
            pltpu.VMEM(piece, BF16),
            pltpu.VMEM(piece, BF16),
            pltpu.VMEM(piece, BF16),
            pltpu.VMEM(piece, BF16),
            pltpu.VMEM(piece, BF16),
            pltpu.VMEM((GROUPS, MINE * 128, 256), F32),
            pltpu.VMEM((PART * TILES, 128), F32),
            pltpu.VMEM((GROUPS, TILES, PART, 128), BF16),
            pltpu.VMEM((GROUPS, CH, PART, 128), BF16),
            pltpu.VMEM((CH, 2, 64, HALF), BF16),
            pltpu.VMEM((128, CH * PART), BF16),
            pltpu.VMEM((128, HALF), F32),
            pltpu.VMEM((TILES, 128, LANES), BF16),
            dma((11,)),
            dma((2,)),
            dma((3, GROUPS)),
            dma((3, GROUPS)),
            dma((1,)),
            dma((CH,)),
            dma((CH,)),
            dma((1,)),
            dma((1,)),
            dma((1,)),
            dma((GROUPS,)),
            dma((GROUPS,)),
            dma((1,)),
            dma((1,)),
        ],
        compiler_params=pltpu.CompilerParams(
            collective_id=0, has_side_effects=True, vmem_limit_bytes=60 * 1024 * 1024
        ),
        cost_estimate=pl.CostEstimate(flops=3_000_000_000, bytes_accessed=4_000_000, transcendentals=0),
    )(
        query, key_in, value, short_taps, filt, skip_gain.reshape(1, LANES), out_weight,
        jnp.asarray(squares), jnp.asarray(finals), jnp.asarray(twiddles),
    )


def solution(mesh):
    return jax.shard_map(
        per_device,
        mesh=mesh,
        in_specs=(
            P("ctx", "ch"),
            P("ctx", "ch"),
            P("ctx", "ch"),
            P(None, None, "ch"),
            P("ctx", "ch"),
            P("ch"),
            P("ch", None),
        ),
        out_specs=P("ctx", "ch"),
        check_vma=False,
    )
```

```python
import functools

import jax
import jax.numpy as jnp
import ml_dtypes
import numpy as np
from jax import lax
from jax.experimental import pallas as pl
from jax.experimental.pallas import tpu as pltpu
from jax.sharding import PartitionSpec as P

CTX = 16
CH = 16
ROWS = 1024
LANES = 128
TILES = ROWS // 128
OWN = LANES // CTX
HALF = 1024
GROUPS = 2
PART = LANES // GROUPS
MINE = OWN // GROUPS
PIECE = MINE * TILES
F32 = jnp.float32
BF16 = jnp.bfloat16
MESH = pl.DeviceIdType.MESH


def hi_lo(matrix):
    high = matrix.astype(ml_dtypes.bfloat16)
    low = (matrix - high.astype(np.float64)).astype(ml_dtypes.bfloat16)
    return high, low


def transform_matrices():
    index = np.arange(128, dtype=np.float64)
    shifted = index + 0.25
    turn = 2.0 * np.pi
    first = turn * np.outer(shifted, index) / 128.0
    forward = np.concatenate([np.cos(first), -np.sin(first)], axis=0)
    first_hi, first_lo = hi_lo(forward)
    first_cat = np.concatenate([first_hi, first_lo], axis=1)
    twiddle = turn * np.outer(shifted, index) / 16384.0
    twiddles = np.stack([np.cos(twiddle), -np.sin(twiddle)]).astype(np.float32)
    second = turn * np.outer(index, index) / 128.0
    cos, sin = np.cos(second), np.sin(second)
    ahead = np.block([[cos, -sin], [sin, cos]])
    back = np.block([[cos, sin], [-sin, cos]])
    last = np.concatenate([np.cos(first).T, -np.sin(first).T], axis=1) / 16384.0
    squares = np.stack([first_cat, *hi_lo(ahead), *hi_lo(back)])
    finals = np.stack(hi_lo(last))
    return squares, finals, twiddles


def split(value):
    high = value.astype(BF16)
    return high, (value - high.astype(F32)).astype(BF16)


def mul(a, b):
    return jnp.dot(a, b, preferred_element_type=F32)


def spectrum(channels, squares, tw_re, tw_im):
    points = jnp.concatenate(channels, axis=1).astype(BF16)
    stage = mul(squares[0], jnp.concatenate([points, points], axis=0))
    parts = []
    for i in range(len(channels)):
        re, im = stage[:128, 128 * i : 128 * i + 128], stage[128:, 128 * i : 128 * i + 128]
        parts.append(jnp.concatenate([re * tw_re - im * tw_im, re * tw_im + im * tw_re], axis=1))
    high, low = split(jnp.concatenate(parts, axis=0))
    return mul(high, squares[1]) + mul(low, squares[1]) + mul(high, squares[2])


def causal(signal, response, squares, finals, tw_re, tw_im):
    s_re, s_im = signal[:, :128], signal[:, 128:]
    r_re, r_im = response[:, :128], response[:, 128:]
    high, low = split(
        jnp.concatenate([s_re * r_re - s_im * r_im, s_re * r_im + s_im * r_re], axis=1)
    )
    stage = mul(high, squares[3]) + mul(low, squares[3]) + mul(high, squares[4])
    turned = []
    for i in range(signal.shape[0] // 128):
        re, im = stage[128 * i : 128 * i + 128, :128], stage[128 * i : 128 * i + 128, 128:]
        turned.append(jnp.concatenate([re * tw_re + im * tw_im, im * tw_re - re * tw_im], axis=0))
    high, low = split(jnp.concatenate(turned, axis=1))
    return mul(finals[0], high) + mul(finals[0], low) + mul(finals[1], high)


def kernel(
    q_hbm, k_hbm, v_hbm, taps_hbm, filt_hbm, skip_hbm, w_hbm, sq_hbm, fin_hbm, tw_hbm,
    out_hbm,
    q_in, k_in, v_in, taps, filt, skip, squares, finals, twiddle,
    ext, halo_out, halo_in, filt_t, gate_t, product_t, skipped_t,
    f_out, p_out, y_out, f_in, p_in, y_in,
    response, rows_t, hidden, hidden_in, weights, lhs, total, mixed,
    load_sem, halo_sem, send_sem, recv_sem, w_send, w_recv, y_recv, x_recv, core_send, core_recv,
    h_send, h_recv, o_send, o_recv,
):
    c, h = lax.axis_index("ctx"), lax.axis_index("ch")
    core = lax.rem(c, 2)
    sibling = c + 1 - 2 * core
    y = c // 4
    zb, at = h // 8, lax.rem(h, 8)
    za, x = at // 4, lax.rem(h, 4)
    across = (1 - zb) * 8 + at
    beside = zb * 8 + (1 - za) * 4 + x
    diagonal = (1 - zb) * 8 + (1 - za) * 4 + x

    loads = [
        pltpu.make_async_copy(src, dst, load_sem.at[i])
        for i, (src, dst) in enumerate(
            [
                (filt_hbm, filt), (k_hbm, k_in), (v_hbm, v_in), (q_hbm, q_in), (taps_hbm, taps),
                (skip_hbm, skip), (sq_hbm, squares), (fin_hbm, finals), (tw_hbm, twiddle),
                (w_hbm.at[pl.ds(0, 64), pl.ds(pl.multiple_of(zb * HALF, HALF), HALF)], weights.at[h, 0]),
                (w_hbm.at[pl.ds(64, 64), pl.ds(pl.multiple_of(zb * HALF, HALF), HALF)], weights.at[h, 1]),
            ]
        )
    ]
    loads[0].start()

    barrier = pltpu.get_barrier_semaphore()

    @pl.loop(1, 16)
    def _(step):
        pl.semaphore_signal(
            barrier, inc=1, device_id={"ctx": lax.rem(c + step, CTX)}, device_id_type=MESH
        )

    @pl.loop(1, 16)
    def _(step):
        pl.semaphore_signal(
            barrier, inc=1, device_id={"ch": lax.rem(h + step, CH)}, device_id_type=MESH
        )

    for load in loads[1:]:
        load.start()

    def turn(target, tile, value):
        target[pl.ds(tile, LANES, stride=TILES), :] = value.T

    def pack(target, source):
        for g in range(GROUPS):
            rows = source[PART * TILES * g : PART * TILES * (g + 1), :]
            target[g] = rows.reshape(CTX, PIECE, 128).astype(BF16)

    def exchange(kind, g, source, target, step):
        peer = lax.rem(c + step, CTX)
        return pltpu.make_async_remote_copy(
            src_ref=source.at[g, peer], dst_ref=target.at[g, c],
            send_sem=send_sem.at[kind, g], recv_sem=recv_sem.at[kind, g],
            device_id={"ctx": peer}, device_id_type=MESH,
        )

    def sum_of(part, send, recv):
        return pltpu.make_async_remote_copy(
            src_ref=part, dst_ref=part, send_sem=send, recv_sem=recv,
            device_id={"ctx": sibling}, device_id_type=MESH,
        )

    def pieces(kind, g, target):
        return sum_of(target.at[g, pl.ds(0, CTX - 1)], send_sem.at[kind, g], recv_sem.at[kind, g])

    def start_exchange(kind, g, source, target):
        @pl.loop(1, CTX)
        def _(step):
            exchange(kind, g, source, target, step).start()

        target[g, c] = source[g, c]

    def wait_exchange(kind, g, target):
        pieces(kind, g, target).wait_recv()

    column = (h, across, beside, diagonal)

    def quarter(block, q):
        return weights.at[block, core, pl.ds(pl.multiple_of(16 * q, 16), 16)]

    def along_z(i):
        half = zb if i == 1 else 1 - zb
        return pltpu.make_async_remote_copy(
            src_ref=w_hbm.at[
                pl.ds(pl.multiple_of(core * 64 + y * 16, 16), 16),
                pl.ds(pl.multiple_of(half * HALF, HALF), HALF),
            ],
            dst_ref=quarter(h, y), send_sem=w_send.at[0], recv_sem=w_recv.at[h],
            device_id={"ch": column[i + 1]}, device_id_type=MESH,
        )

    def along_y(block, step, low):
        peer = lax.rem(y + step, 4)
        return pltpu.make_async_remote_copy(
            src_ref=quarter(block, y), dst_ref=quarter(block, y),
            send_sem=w_send.at[0], recv_sem=y_recv.at[block] if low else y_recv.at[y],
            device_id={"ctx": 4 * peer + lax.rem(c, 4)}, device_id_type=MESH,
        )

    def along_x(block, step, whole):
        peer = lax.rem(x + step, 4)
        part = weights.at[block, core] if whole else quarter(block, y)
        return pltpu.make_async_remote_copy(
            src_ref=part, dst_ref=part, send_sem=w_send.at[0],
            recv_sem=x_recv.at[0] if whole else w_recv.at[block],
            device_id={"ch": (h // 4) * 4 + peer}, device_id_type=MESH,
        )

    def wait_quarter(block):
        sum_of(quarter(block, y), w_send.at[0], w_recv.at[block]).wait_recv()

    def on_core(which):
        return pl.when(core == which)

    def steps_of_four(body):
        pl.loop(1, 4)(body)

    def other_columns(body):
        @pl.loop(1, 4)
        def _(step):
            peer = lax.rem(x + step, 4)

            @pl.loop(0, 4)
            def _(z):
                body(4 * z + peer)

    def weights_start():
        for i in range(3):
            along_z(i).start()

        @on_core(0)
        def _():
            steps_of_four(lambda step: along_x(h, step, True).start())

        @on_core(1)
        def _():
            steps_of_four(lambda step: along_x(h, step, False).start())

    def weights_second():
        for block in column[1:]:
            wait_quarter(block)

            @on_core(0)
            def _():
                steps_of_four(lambda step: along_y(block, step, True).start())

            @on_core(1)
            def _():
                steps_of_four(lambda step: along_x(block, step, False).start())

    def weights_third():
        @on_core(0)
        def _():
            for block in column[1:]:
                three = weights.at[block, core, pl.ds(0, 48)]
                sum_of(three, w_send.at[0], y_recv.at[block]).wait_recv()
                steps_of_four(lambda step: along_x(block, step, True).start())

        @on_core(1)
        def _():
            for block in column[1:]:
                steps_of_four(lambda step: along_y(block, step, False).start())

            def onward(block):
                wait_quarter(block)
                steps_of_four(lambda step: along_y(block, step, False).start())

            other_columns(onward)

    def weights_gathered():
        @on_core(0)
        def _():
            sum_of(weights.at[pl.ds(0, 12), core], w_send.at[0], x_recv.at[0]).wait_recv()

        @on_core(1)
        def _():
            @pl.loop(1, 4)
            def _(step):
                part = weights.at[pl.ds(0, CH - 1), core, pl.ds(0, 16)]
                sum_of(part, w_send.at[0], y_recv.at[lax.rem(y + step, 4)]).wait_recv()

    def weights_drain():
        sum_of(weights.at[pl.ds(0, CH - 1), core], w_send.at[0], x_recv.at[0]).wait_send()

    def core_copy(block):
        return pltpu.make_async_remote_copy(
            src_ref=weights.at[block, core], dst_ref=weights.at[block, core],
            send_sem=core_send.at[0], recv_sem=core_recv.at[0],
            device_id={"ctx": sibling}, device_id_type=MESH,
        )

    def core_sum():
        return sum_of(weights.at[pl.ds(0, CH - 1), 1 - core], core_send.at[0], core_recv.at[0])

    loads[0].wait()
    for tile in range(TILES):
        turn(filt_t, tile, filt[128 * tile : 128 * tile + 128, :])
    pack(f_out, filt_t)

    for load in loads[1:]:
        load.wait()
    for i, source in enumerate((k_in, v_in, q_in)):
        halo_out[16 * i : 16 * i + 16, :] = source[ROWS - 16 :, :]

    def smooth(tile):
        first = 128 * tile + 8
        sums = []
        for i, which in enumerate((1, 2, 0)):
            part = taps[0, which : which + 1, :] * ext[i, first : first + 128, :]
            part += taps[1, which : which + 1, :] * ext[i, first - 1 : first + 127, :]
            part += taps[2, which : which + 1, :] * ext[i, first - 2 : first + 126, :]
            sums.append(part)
        both = sums[0] * sums[1]
        turn(product_t, tile, both)
        turn(skipped_t, tile, skip[...] * both)
        turn(gate_t, tile, sums[2])

    pl.semaphore_wait(barrier, 30)

    halo = pltpu.make_async_remote_copy(
        src_ref=halo_out, dst_ref=halo_in, send_sem=halo_sem.at[0], recv_sem=halo_sem.at[1],
        device_id={"ctx": lax.rem(c + 1, CTX)}, device_id_type=MESH,
    )
    halo.start()
    for g in range(GROUPS):
        start_exchange(0, g, f_out, f_in)
    weights_start()

    for i, source in enumerate((k_in, v_in, q_in)):
        ext[i, 8:, :] = source[...].astype(F32)
    for tile in range(1, TILES):
        smooth(tile)

    halo.wait()
    for i in range(3):
        before = halo_in[16 * i : 16 * i + 16, :].astype(F32)[8:]
        ext[i, :8, :] = jnp.where(c == 0, jnp.zeros_like(before), before)
    smooth(0)
    pack(p_out, product_t)
    for g in range(GROUPS):
        start_exchange(1, g, p_out, p_in)


    tw_re, tw_im = twiddle[0], twiddle[1]

    def channels(source, g):
        parts = source[g].astype(F32)
        return [parts[:, 8 * i : 8 * i + 8, :].reshape(128, 128) for i in range(MINE)]

    for g in range(GROUPS):
        wait_exchange(0, g, f_in)
        response[g] = spectrum(channels(f_in, g), squares, tw_re, tw_im)

    weights_second()
    for g in range(GROUPS):
        wait_exchange(1, g, p_in)
        signal = spectrum(channels(p_in, g), squares, tw_re, tw_im)
        conv = causal(signal, response[g], squares, finals, tw_re, tw_im)
        rows = [conv[:, 128 * i : 128 * i + 128].reshape(CTX, TILES, 128) for i in range(MINE)]
        y_out[g] = jnp.concatenate(rows, axis=1).astype(BF16)
        start_exchange(2, g, y_out, y_in)

    weights_third()
    def hidden_copy(g, half, tile):
        peer = 8 * half + tile
        return pltpu.make_async_remote_copy(
            src_ref=hidden.at[g, tile], dst_ref=hidden_in.at[g, h],
            send_sem=h_send.at[g], recv_sem=h_recv.at[g],
            device_id={"ch": peer}, device_id_type=MESH,
        )

    for g in range(GROUPS):
        wait_exchange(2, g, y_in)
        for fourth in range(4):
            rows = slice(PART * TILES // 4 * fourth, PART * TILES // 4 * (fourth + 1))
            whole = slice(PART * TILES * g + rows.start, PART * TILES * g + rows.stop)
            conv = y_in[g, 4 * fourth : 4 * fourth + 4].astype(F32).reshape(4 * PIECE, 128)
            rows_t[rows, :] = gate_t[whole, :] * (conv + skipped_t[whole, :])

        @pl.loop(0, TILES)
        def _(step):
            tile = lax.rem(at + step, TILES)
            value = rows_t[pl.ds(tile, PART, stride=TILES), :].astype(BF16)
            hidden[g, tile] = value
            hidden_copy(g, 1 - zb, tile).start()

            @pl.when(step == 0)
            def _():
                hidden_in[g, h] = value

            @pl.when(step > 0)
            def _():
                hidden_copy(g, zb, tile).start()

    weights_gathered()

    @pl.loop(1, CH)
    def _(step):
        core_copy(lax.rem(h + step, CH)).start()

    core_sum().wait_recv()

    def mixed_copy(tile):
        return pltpu.make_async_remote_copy(
            src_ref=mixed.at[tile], dst_ref=out_hbm.at[pl.ds(pl.multiple_of(128 * at, 128), 128), :],
            send_sem=o_send.at[0], recv_sem=o_recv.at[0],
            device_id={"ch": 8 * zb + tile}, device_id_type=MESH,
        )

    own_copy = pltpu.make_async_copy(
        mixed.at[at], out_hbm.at[pl.ds(pl.multiple_of(128 * at, 128), 128), :], load_sem.at[0]
    )

    def hidden_sum(g):
        return sum_of(hidden_in.at[g, pl.ds(0, CH - 1)], h_send.at[g], h_recv.at[g])

    for g in range(GROUPS):
        hidden_sum(g).wait_recv()
        many = 128 // PART
        for i in range(CH // many):
            block = hidden_in[g, many * i : many * i + many].astype(F32).reshape(128, 128)
            lhs[:, 128 * i : 128 * i + 128] = block.T.astype(BF16)

        for part in range(4):
            cut = slice(256 * part, 256 * part + 256)
            side, first = 2 * g // GROUPS, PART * g % 64
            rhs = weights[:, side, first : first + PART, cut].reshape(CH * PART, 256)
            value = mul(lhs[...], rhs)
            if g > 0:
                value += total[:, cut]
            if g < GROUPS - 1:
                total[:, cut] = value
                continue
            value = value.astype(BF16)
            for i in range(2):
                tile = 2 * part + i
                mixed[tile] = value[:, 128 * i : 128 * i + 128]

                @pl.when(at != tile)
                def _():
                    mixed_copy(tile).start()

                @pl.when(at == tile)
                def _():
                    own_copy.start()

    for g in range(GROUPS):
        for kind, target in enumerate((f_in, p_in, y_in)):
            pieces(kind, g, target).wait_send()
        hidden_sum(g).wait_send()
    weights_drain()
    core_sum().wait_send()
    seven = sum_of(mixed.at[pl.ds(0, TILES - 1)], o_send.at[0], o_recv.at[0])
    seven.wait_send()
    seven.wait_recv()
    own_copy.wait()


def per_device(query, key_in, value, short_taps, filt, skip_gain, out_weight):
    squares, finals, twiddles = transform_matrices()
    in_hbm = pl.BlockSpec(memory_space=pltpu.HBM)
    dma = pltpu.SemaphoreType.DMA
    piece = (GROUPS, CTX, PIECE, 128)
    return pl.pallas_call(
        kernel,
        out_shape=jax.ShapeDtypeStruct((ROWS, LANES), BF16),
        in_specs=[in_hbm] * 10,
        out_specs=in_hbm,
        scratch_shapes=[
            pltpu.VMEM((ROWS, LANES), BF16),
            pltpu.VMEM((ROWS, LANES), BF16),
            pltpu.VMEM((ROWS, LANES), BF16),
            pltpu.VMEM((3, 3, LANES), F32),
            pltpu.VMEM((ROWS, LANES), F32),
            pltpu.VMEM((1, LANES), F32),
            pltpu.VMEM(squares.shape, BF16),
            pltpu.VMEM(finals.shape, BF16),
            pltpu.VMEM(twiddles.shape, F32),
            pltpu.VMEM((3, ROWS + 8, LANES), F32),
            pltpu.VMEM((48, LANES), BF16),
            pltpu.VMEM((48, LANES), BF16),
            pltpu.VMEM((ROWS, 128), F32),
            pltpu.VMEM((ROWS, 128), F32),
            pltpu.VMEM((ROWS, 128), F32),
            pltpu.VMEM((ROWS, 128), F32),
            pltpu.VMEM(piece, BF16),
            pltpu.VMEM(piece, BF16),
            pltpu.VMEM(piece, BF16),
            pltpu.VMEM(piece, BF16),
            pltpu.VMEM(piece, BF16),
            pltpu.VMEM(piece, BF16),
            pltpu.VMEM((GROUPS, MINE * 128, 256), F32),
            pltpu.VMEM((PART * TILES, 128), F32),
            pltpu.VMEM((GROUPS, TILES, PART, 128), BF16),
            pltpu.VMEM((GROUPS, CH, PART, 128), BF16),
            pltpu.VMEM((CH, 2, 64, HALF), BF16),
            pltpu.VMEM((128, CH * PART), BF16),
            pltpu.VMEM((128, HALF), F32),
            pltpu.VMEM((TILES, 128, LANES), BF16),
            dma((11,)),
            dma((2,)),
            dma((3, GROUPS)),
            dma((3, GROUPS)),
            dma((1,)),
            dma((CH,)),
            dma((CH,)),
            dma((1,)),
            dma((1,)),
            dma((1,)),
            dma((GROUPS,)),
            dma((GROUPS,)),
            dma((1,)),
            dma((1,)),
        ],
        compiler_params=pltpu.CompilerParams(
            collective_id=0, has_side_effects=True, vmem_limit_bytes=60 * 1024 * 1024
        ),
        cost_estimate=pl.CostEstimate(flops=3_000_000_000, bytes_accessed=4_000_000, transcendentals=0),
    )(
        query, key_in, value, short_taps, filt, skip_gain.reshape(1, LANES), out_weight,
        jnp.asarray(squares), jnp.asarray(finals), jnp.asarray(twiddles),
    )


def solution(mesh):
    return jax.shard_map(
        per_device,
        mesh=mesh,
        in_specs=(
            P("ctx", "ch"),
            P("ctx", "ch"),
            P("ctx", "ch"),
            P(None, None, "ch"),
            P("ctx", "ch"),
            P("ch"),
            P("ch", None),
        ),
        out_specs=P("ctx", "ch"),
        check_vma=False,
    )
```
